32 devices in a mesh: dp: 4 (over y, core), expert: 8 (over z, x).
Axes of the slice: x: 2, y: 2, z: 4, core: 2. Of those that a mesh axis runs over, the one named last changes fastest.
Arguments:
- tokens: bfloat16 [4096, 4096], P(('dp', 'expert')), may hold values from -6 to 6
- router_weights: float32 [4096, 8], P(('dp', 'expert')), may hold values from 0.1 to 1
- expert_ids: int32 [4096, 8], P(('dp', 'expert')), may hold values from 0 to 31, as said below
- gate_weight: bfloat16 [32, 4096, 768], P(('dp', 'expert')), may hold values from -0.09375 to 0.09375
- up_weight: bfloat16 [32, 4096, 768], P(('dp', 'expert')), may hold values from -0.09375 to 0.09375
- down_weight: bfloat16 [32, 768, 4096], P(('dp', 'expert')), may hold values from -0.21875 to 0.21875
Outputs:
- mixed: bfloat16 [4096, 4096], P(('dp', 'expert'))
The draws below stay inside these ranges and needn't reach their ends.
Inputs may be any that keep to these rules, and one draw needn't show every extreme that they name: `expert_ids`: each row names 8 different experts. Experts e and e + 8 with e // 8 even form a pair: the 128 tokens of one device (aligned blocks of rows) name the two experts of each pair exactly 2 * 32 times together, and one expert at most 48 times; some expert is named exactly 48 times by the tokens of every device.
All inputs are finite; a program needn't handle non-finite values.
Results may differ from the reference program's by a relative error of at most 0.0058.
Values may be sent and summed in bfloat16 or wider, within the bound.
No kernel may reach another device: no remote copies, remote signals or barrier semaphores. Data moves between devices by JAX's collectives and lax.ppermute only.
A program may use at most 192 MiB of HBM per device.

```python
from functools import partial
import jax
import jax.numpy as jnp
from jax import lax

D = 4096
FF = 768
TOP = 8
TOK_DEV = 128
EXPERTS = 32
GROUP = 8
TOKENS = 4096
MOST = 48


def permute_range(one_key, size):
    return jax.random.permutation(one_key, size).astype(jnp.int32)


def draw_expert_ids(key, part):
    pair_count = EXPERTS // 2
    slot_cap = TOK_DEV * TOP // EXPERTS
    key_list = jax.random.split(key, 7)
    pair_order = jax.vmap(partial(permute_range, size=pair_count))(jax.random.split(key_list[0], EXPERTS))
    rank_table = jax.vmap(partial(permute_range, size=2 * slot_cap))(jax.random.split(key_list[1], EXPERTS * pair_count))
    rank_table = rank_table.reshape(EXPERTS, pair_count, 2 * slot_cap)
    slot_index = jnp.arange(TOK_DEV * TOP, dtype=jnp.int32)
    column = slot_index % pair_count
    occurrence = slot_index // pair_count
    pair = pair_order[:, column]
    hot_pair = jax.random.randint(key_list[2], (pair_count,), 0, 4) == 0
    full_pair = jax.random.randint(key_list[3], (), 0, pair_count)
    cold = jax.random.randint(key_list[4], (EXPERTS, pair_count), slot_cap - slot_cap // 4, slot_cap + slot_cap // 4 + 1)
    warm = jax.random.randint(key_list[5], (EXPERTS, pair_count), 5 * slot_cap // 4, 3 * slot_cap // 2 + 1)
    side_count = jnp.where(hot_pair[None, :], warm, cold)
    side_count = jnp.where(jnp.arange(pair_count)[None, :] == full_pair, 3 * slot_cap // 2, side_count)
    flip = jax.random.randint(key_list[6], (pair_count,), 0, 2)
    sources = jnp.arange(EXPERTS, dtype=jnp.int32)[:, None]
    rank_value = rank_table[sources, pair, occurrence[None, :]]
    count_here = side_count[sources, pair]
    is_high = jnp.where(rank_value < count_here, 1, 0)
    is_high = jnp.where(flip[pair] == 1, 1 - is_high, is_high)
    low_expert = pair // GROUP * 2 * GROUP + pair % GROUP
    chosen = low_expert + GROUP * is_high
    return chosen.reshape(TOKENS, TOP).astype(jnp.int32)


def steps_of(stream_key, dims, shards, least, high):
    factor_of = 1.0
    for axis_at, parts in shards:
        steps = jax.random.uniform(jax.random.fold_in(jax.random.fold_in(stream_key, 6), axis_at), (parts,), jnp.float32, least / len(shards), high / len(shards))
        factor_of = factor_of * jnp.repeat(jnp.exp(steps), dims[axis_at] // parts).reshape((-1,) + (1,) * (len(dims) - 1 - axis_at))
    return factor_of


def bell_draw(key, dims, spread, bound, shards=(), kind=jnp.bfloat16):
    values = spread * jax.random.normal(key, dims, jnp.float32)
    if shards:
        values = values * steps_of(key, dims, shards, -0.22, 0.18)
    return jnp.clip(values, -bound, bound).astype(kind)


def setup_inputs(seed: int = 0) -> dict:
    arg_keys = jax.random.split(jax.random.key(seed), 7)
    return {
        "tokens": bell_draw(arg_keys[0], (TOKENS, D), 1.0, 6.0, ((0, 32),)),
        "router_weights": jnp.clip(0.1 + 0.9 * jax.random.uniform(arg_keys[1], (TOKENS, TOP), jnp.float32) ** steps_of(arg_keys[1], (TOKENS, TOP), ((0, 32),), -0.2, 0.2), 0.1, 1.0),
        "expert_ids": draw_expert_ids(jax.random.fold_in(arg_keys[6], 71), 0),
        "gate_weight": bell_draw(arg_keys[3], (EXPERTS, D, FF), D ** -0.5, 0.09375, ((0, 32),)),
        "up_weight": bell_draw(arg_keys[4], (EXPERTS, D, FF), D ** -0.5, 0.09375, ((0, 32),)),
        "down_weight": bell_draw(arg_keys[5], (EXPERTS, FF, D), FF ** -0.5, 0.21875, ((0, 32),)),
    }


def reference(tokens, router_weights, expert_ids, gate_weight, up_weight, down_weight):
    most_rows = MOST * EXPERTS
    flat_ids = expert_ids.reshape(-1).astype(jnp.int32)
    ordering = jnp.argsort(flat_ids, stable=True).astype(jnp.int32)
    counts = jnp.sum((flat_ids[:, None] == jnp.arange(EXPERTS, dtype=jnp.int32)[None, :]).astype(jnp.int32), axis=0)
    starts = (jnp.cumsum(counts) - counts).astype(jnp.int32)
    padded = jnp.concatenate([ordering, jnp.zeros((most_rows,), jnp.int32)])
    flat_gates = router_weights.reshape(-1)

    def per_expert(summed, expert):
        picked = lax.dynamic_slice_in_dim(padded, starts[expert], most_rows)
        is_valid = jnp.arange(most_rows, dtype=jnp.int32) < counts[expert]
        row_data = tokens[picked // TOP]
        gate_proj = jnp.dot(row_data, gate_weight[expert], preferred_element_type=jnp.float32)
        up_proj = jnp.dot(row_data, up_weight[expert], preferred_element_type=jnp.float32)
        hidden = (jax.nn.silu(gate_proj) * up_proj).astype(jnp.bfloat16)
        result = jnp.dot(hidden, down_weight[expert], preferred_element_type=jnp.float32).astype(jnp.bfloat16)
        weight = jnp.where(is_valid, flat_gates[picked], jnp.zeros_like(flat_gates[picked]))
        summed = summed.at[picked // TOP].add(weight[:, None] * result.astype(jnp.float32))
        return summed, None

    summed, unused = lax.scan(per_expert, jnp.zeros((TOKENS, D), jnp.float32), jnp.arange(EXPERTS, dtype=jnp.int32))
    return summed.astype(jnp.bfloat16)
```

```python
import jax
import jax.numpy as jnp
from jax import lax
from jax.sharding import Mesh, PartitionSpec as P

F32 = jnp.float32
BF16 = jnp.bfloat16
EXTRA = 128


def arrivals(n):
    order = []
    for i in range(n):
        found = []
        for r in range(1, n):
            sides = [(r, -r)] if i - r >= 0 else []
            if i + r < n:
                sides = sides + [(r, r)] if i % 2 else [(r, r)] + sides
            found += sides
        order.append(found)
    return order


def pick(index, values):
    out = values[-1]
    for i in range(len(values) - 2, -1, -1):
        if values[i] is not out:
            out = jnp.where(index == i, values[i], out)
    return out


def shifted(n, by):
    return [(i, i + by) for i in range(n) if 0 <= i + by < n]


def places(ids, plane_ids):
    chosen = jnp.any(ids[:, :, None, None] == plane_ids[None, None], axis=1)
    ones = chosen.astype(F32)
    tokens = ids.shape[0]
    before = (jnp.arange(tokens)[:, None] > jnp.arange(tokens)[None, :]).astype(F32)
    rank = jnp.einsum("ts,sjc->tjc", before, ones, preferred_element_type=F32)
    low_count = jnp.sum(ones[:, :, 0], axis=0)
    rank = rank + jnp.stack([jnp.zeros_like(low_count), low_count], axis=-1)[None]
    return jnp.where(chosen, rank, -1.0)


def local(tokens, router_weights, expert_ids, gate_weight, up_weight, down_weight):
    z_size = lax.axis_size("z")
    x_size = lax.axis_size("x")
    y_size = lax.axis_size("y")
    lane_count = z_size * x_size
    chips = y_size * x_size
    count, width = tokens.shape
    top = expert_ids.shape[1]
    rows = count * top * 2 // (2 * y_size * lane_count)
    z_at = lax.axis_index("z")
    core = lax.axis_index("core")

    chip = jnp.arange(chips, dtype=jnp.int32)
    low = 2 * (chip // x_size) * lane_count + z_at * x_size + chip % x_size
    plane_ids = jnp.stack([low, low + lane_count], axis=-1).astype(F32)
    own_chip = lax.axis_index("y") * x_size + lax.axis_index("x")
    low_here = jnp.take(low, own_chip).astype(F32)
    high_here = low_here + lane_count

    swap = [(0, 1), (1, 0)]
    weights = [(gate_weight[0], up_weight[0], down_weight[0])]
    weights.append(tuple(lax.ppermute(w, "core", swap) for w in weights[0]))

    hi = router_weights.astype(BF16)
    rest = router_weights - hi.astype(F32)
    mid = rest.astype(BF16)
    last = (rest - mid.astype(F32)).astype(BF16)
    block = jnp.concatenate(
        [tokens, expert_ids.astype(BF16), hi, mid, last, jnp.zeros((count, EXTRA - 4 * top), BF16)], axis=1
    )

    order = arrivals(z_size)
    moving_up, moving_down = {0: block}, {0: block}
    for r in range(1, z_size):
        moving_up[r] = lax.ppermute(moving_up[r - 1], "z", shifted(z_size, 1))
        moving_down[r] = lax.ppermute(moving_down[r - 1], "z", shifted(z_size, -1))

    def slot_of(k):
        if k == 0:
            return block
        values = []
        for i in range(z_size):
            r, offset = order[i][k - 1]
            values.append(moving_up[r] if offset < 0 else moving_down[r])
        return pick(z_at, values)

    row = jnp.arange(rows, dtype=jnp.int32).astype(F32)
    sums = []
    for k in range(z_size):
        held = slot_of(k)
        extra = held[:, width:].astype(F32)
        rank = places(extra[:, :top], plane_ids)
        hit = rank[:, :, :, None] == row
        taken = jnp.any(hit, axis=2).reshape(count, chips * rows).astype(BF16)
        sent = lax.dot_general(taken, held, (((0,), (0,)), ((), ())), preferred_element_type=F32).astype(BF16)
        arrived = lax.all_to_all(sent.reshape(chips, rows, width + EXTRA), ("y", "x"), 0, 0, tiled=True)
        ids_here = arrived[:, :, width : width + top].astype(F32)
        has_low = jnp.any(ids_here == low_here, axis=-1)
        has_both = has_low & jnp.any(ids_here == high_here, axis=-1)
        low_rows = jnp.sum(has_low.astype(F32), axis=1) - 0.5 * jnp.sum(has_both.astype(F32), axis=1)
        is_low = (row[None, :] < low_rows[:, None]).reshape(-1)
        data = arrived.reshape(-1, width + EXTRA)[:, :width]
        out = None
        for which in range(2):
            w_gate, w_up, w_down = weights[which]
            mine = is_low == (core == which)
            gate = jnp.dot(data, w_gate, preferred_element_type=F32)
            up = jnp.dot(data, w_up, preferred_element_type=F32)
            hidden = jnp.where(mine[:, None], jax.nn.silu(gate) * up, 0.0).astype(BF16)
            part = jnp.dot(hidden, w_down, preferred_element_type=F32)
            out = part if out is None else out + part
        back = lax.all_to_all(out.astype(BF16).reshape(chips, rows, width), ("y", "x"), 0, 0, tiled=True)
        back = back.reshape(-1, width)
        total = None
        same = extra[:, :top, None, None] == plane_ids[None, None]
        for part in range(2):
            w_part = extra[:, (1 + part) * top : (2 + part) * top]
            w_of = jnp.sum(jnp.where(same, w_part[:, :, None, None], 0.0), axis=1)
            mix = jnp.sum(jnp.where(hit, w_of[..., None], 0.0), axis=2).reshape(count, chips * rows).astype(BF16)
            term = jnp.dot(mix, back, preferred_element_type=F32)
            total = term if total is None else total + term
        sums.append(total)

    from_below = from_above = None
    for r in range(z_size - 1, 0, -1):
        ups, downs = [], []
        for i in range(z_size):
            offsets = [offset for _, offset in order[i]]
            ups.append(sums[1 + offsets.index(r)] if r in offsets else None)
            downs.append(sums[1 + offsets.index(-r)] if -r in offsets else None)
        ups = [u if u is not None else next(v for v in ups if v is not None) for u in ups]
        downs = [u if u is not None else next(v for v in downs if v is not None) for u in downs]
        up, down = pick(z_at, ups), pick(z_at, downs)
        if from_below is not None:
            up = up + from_below.astype(F32)
            down = down + from_above.astype(F32)
        from_below = lax.ppermute(up.astype(BF16), "z", [(i, i + 1) for i in range(z_size) if i + r < z_size])
        from_above = lax.ppermute(down.astype(BF16), "z", [(i, i - 1) for i in range(z_size) if i - r >= 0])
    mixed = sums[0]
    if from_below is not None:
        mixed = mixed + from_below.astype(F32) + from_above.astype(F32)
    return mixed.astype(BF16)


def solution(mesh):
    groups, lanes = mesh.shape["dp"], mesh.shape["expert"]
    y_size = groups // 2
    x_size = y_size if lanes % y_size == 0 else 1
    fine = Mesh(mesh.devices.reshape(y_size, 2, lanes // x_size, x_size), ("y", "core", "z", "x"))
    split = ("y", "core", "z", "x")
    return jax.shard_map(
        local,
        mesh=fine,
        in_specs=(P(split, None), P(split, None), P(split, None), P(split, None, None), P(split, None, None), P(split, None, None)),
        out_specs=P(split, None),
        check_vma=False,
    )
```

```python
from functools import partial

import jax
import jax.numpy as jnp
from jax import lax
from jax.experimental import pallas as pl
from jax.experimental.pallas import tpu as pltpu
from jax.sharding import Mesh, PartitionSpec as P

F32 = jnp.float32
BF16 = jnp.bfloat16
EXTRA = 128
MIB = 2**20


def divisor(size, most):
    return next(d for d in range(min(size, most), 0, -1) if size % d == 0)


def experts_kernel(info, x_ref, g0, u0, d0, g1, u1, d1, o_ref, bg0, bu0, bd0, bg1, bu1, bd1, gate_ref, hid, sems, *, rows, top, tile, span):
    total, width = o_ref.shape
    ff = g0.shape[1]
    pairs = ((g0, bg0), (u0, bu0), (g1, bg1), (u1, bu1), (d0, bd0), (d1, bd1))
    copies = [pltpu.make_async_copy(src, dst, sems.at[n]) for n, (src, dst) in enumerate(pairs)]
    for c in copies:
        c.start()

    ids = x_ref[:, width:].astype(F32)
    is_id = lax.broadcasted_iota(jnp.int32, ids.shape, 1) < top
    low, high, flip = info[0].astype(F32), info[1].astype(F32), info[2].astype(F32)
    has_low = jnp.max(jnp.where(is_id & (ids == low), 1.0, 0.0), axis=1, keepdims=True)
    has_high = jnp.max(jnp.where(is_id & (ids == high), 1.0, 0.0), axis=1, keepdims=True)
    share = jnp.broadcast_to(has_low * (1.0 - 0.5 * has_high), (total, 128)).astype(BF16)
    r = lax.broadcasted_iota(jnp.int32, (total, total), 0)
    c = lax.broadcasted_iota(jnp.int32, (total, total), 1)
    same = jnp.where(r // rows == c // rows, 1.0, 0.0).astype(BF16)
    low_rows = jnp.dot(same, share, preferred_element_type=F32)
    at = (lax.broadcasted_iota(jnp.int32, (total, 128), 0) % rows).astype(F32)
    is_low = jnp.where(at < low_rows, 1.0, 0.0)
    first = (is_low * (1.0 - flip) + (1.0 - is_low) * flip)[:, :1]

    for which, (bg, bu) in enumerate(((bg0, bu0), (bg1, bu1))):
        keep = first if which == 0 else 1.0 - first
        copies[2 * which].wait()

        @pl.loop(0, ff // tile)
        def _(t):
            s = pl.ds(pl.multiple_of(t * tile, tile), tile)
            gate_ref[:, s] = jnp.dot(x_ref[:, :width], bg[:, s], preferred_element_type=F32)

        copies[2 * which + 1].wait()

        @pl.loop(0, ff // tile)
        def _(t):
            s = pl.ds(pl.multiple_of(t * tile, tile), tile)
            up = jnp.dot(x_ref[:, :width], bu[:, s], preferred_element_type=F32)
            gate = gate_ref[:, s]
            h = jnp.where(keep > 0.5, gate / (1.0 + jnp.exp(-gate)) * up, 0.0)
            hid[:, pl.ds(pl.multiple_of(which * ff + t * tile, tile), tile)] = h.astype(BF16)

    copies[4].wait()
    copies[5].wait()

    @pl.loop(0, width // span)
    def _(n):
        s = pl.ds(pl.multiple_of(n * span, span), span)
        o_ref[:, s] = (
            jnp.dot(hid[:, :ff], bd0[:, s], preferred_element_type=F32)
            + jnp.dot(hid[:, ff:], bd1[:, s], preferred_element_type=F32)
        ).astype(BF16)


def experts_apply(info, x, first, second, rows, top):
    width, ff = first[0].shape
    total = x.shape[0]
    weights = [pltpu.VMEM(w.shape, BF16) for w in first + second]
    return pl.pallas_call(
        partial(experts_kernel, rows=rows, top=top, tile=divisor(ff // 128, 2) * 128, span=divisor(width // 128, 4) * 128),
        out_shape=jax.ShapeDtypeStruct((total, width), BF16),
        grid_spec=pltpu.PrefetchScalarGridSpec(
            num_scalar_prefetch=1,
            grid=(1,),
            in_specs=[pl.BlockSpec(x.shape, lambda i, s: (0, 0))] + [pl.BlockSpec(memory_space=pl.ANY)] * 6,
            out_specs=pl.BlockSpec((total, width), lambda i, s: (0, 0)),
            scratch_shapes=weights
            + [pltpu.VMEM((total, ff), F32), pltpu.VMEM((total, 2 * ff), BF16), pltpu.SemaphoreType.DMA((6,))],
        ),
        compiler_params=pltpu.CompilerParams(vmem_limit_bytes=54 * MIB),
        cost_estimate=pl.CostEstimate(
            flops=12 * total * width * ff, bytes_accessed=12 * width * ff + 4 * total * width, transcendentals=2 * total * ff
        ),
    )(info, x, *first, *second)


def places(ids, plane_ids):
    chosen = jnp.any(ids[:, :, None, None] == plane_ids[None, None], axis=1)
    ones = chosen.astype(F32)
    tokens = ids.shape[0]
    before = (jnp.arange(tokens)[:, None] > jnp.arange(tokens)[None, :]).astype(F32)
    rank = jnp.einsum("ts,sjc->tjc", before, ones, preferred_element_type=F32)
    low_count = jnp.sum(ones[:, :, 0], axis=0)
    rank = rank + jnp.stack([jnp.zeros_like(low_count), low_count], axis=-1)[None]
    return jnp.where(chosen, rank, -1.0)


def after(value, *others):
    return lax.optimization_barrier((value,) + others)[0]


def local(tokens, router_weights, expert_ids, gate_weight, up_weight, down_weight):
    z_size = lax.axis_size("z")
    x_size = lax.axis_size("x")
    y_size = lax.axis_size("y")
    lane_count = z_size * x_size
    chips = y_size * x_size
    count, width = tokens.shape
    top = expert_ids.shape[1]
    rows = count * top // (y_size * lane_count)
    z_at = lax.axis_index("z")

    chip = jnp.arange(chips, dtype=jnp.int32)
    low = 2 * (chip // x_size) * lane_count + z_at * x_size + chip % x_size
    plane_ids = jnp.stack([low, low + lane_count], axis=-1).astype(F32)
    low_here = 2 * lax.axis_index("y") * lane_count + z_at * x_size + lax.axis_index("x")
    info = jnp.stack([low_here, low_here + lane_count, lax.axis_index("core")]).astype(jnp.int32)

    def flip(value, mask):
        return lax.ppermute(value, "z", [(i, i ^ mask) for i in range(z_size)])

    hi = router_weights.astype(BF16)
    mid = (router_weights - hi.astype(F32)).astype(BF16)
    block = jnp.concatenate(
        [tokens, expert_ids.astype(BF16), hi, mid, jnp.zeros((count, EXTRA - 3 * top), BF16)], axis=1
    )

    swap = [(0, 1), (1, 0)]
    own = [gate_weight[0], up_weight[0], down_weight[0]]
    other = [lax.ppermute(w, "core", swap) for w in own]

    row = jnp.arange(rows, dtype=jnp.int32).astype(F32)

    def routed(part):
        extra = part[:, width:].astype(F32)
        rank = places(extra[:, :top], plane_ids)
        hit = rank[:, :, :, None] == row
        taken = jnp.any(hit, axis=2).reshape(count, chips * rows).astype(BF16)
        same = extra[:, :top, None, None] == plane_ids[None, None]
        mixes = []
        for n in (1, 2):
            w_of = jnp.sum(jnp.where(same, extra[:, n * top : (n + 1) * top, None, None], 0.0), axis=1)
            mixes.append(jnp.sum(jnp.where(hit, w_of[..., None], 0.0), axis=2).reshape(count, chips * rows).astype(BF16))
        return taken, mixes

    def exchange(value):
        moved = lax.all_to_all(value.reshape(chips, rows, value.shape[1]), ("y", "x"), 0, 0, tiled=True)
        return moved.reshape(value.shape)

    def gather(part, taken):
        return lax.dot_general(taken, part, (((0,), (0,)), ((), ())), preferred_element_type=F32).astype(BF16)

    def run(k, *others):
        outs[k] = experts_apply(info, after(arrived[k], *others), own, other, rows, top)

    moving = {k: flip(block, k) for k in range(1, z_size) if k & (k - 1) == 0}
    held, mixes, sent, arrived, outs = {0: block}, {}, {}, {}, {}
    for k in range(z_size):
        if k:
            bit = k & -k
            held[k] = after(moving[k] if k == bit else flip(held[k ^ bit], bit), sent[k - 1])
        taken, mixes[k] = routed(held[k])
        sent[k] = gather(held[k], taken)
        if k:
            sent[k] = after(sent[k], arrived[k - 1], *[outs[o] for o in outs if o == k - 3])
        if k >= 2:
            run(k - 2, sent[k])
        arrived[k] = exchange(sent[k])
    last = z_size - 1
    run(last, *[outs[o] for o in outs if o == last - 2])
    if last:
        run(last - 1, outs[last])

    sums, back, backs = {}, None, {}
    for k in range(last, -1, -1):
        source = outs[k] if back is None else after(outs[k], back)
        if back is not None:
            backs[k + 1] = after(back, source)
        back = exchange(source)
    backs[0] = back
    for k in range(last, -1, -1):
        sums[k] = sum(jnp.dot(mix, backs[k], preferred_element_type=F32) for mix in mixes[k])
    mask = 1
    while mask < z_size:
        for o in sorted(sums, reverse=True):
            if o & mask:
                sums[o ^ mask] = sums[o ^ mask] + flip(sums.pop(o).astype(BF16), mask).astype(F32)
        mask *= 2
    return sums[0].astype(BF16)


def solution(mesh):
    groups, lanes = mesh.shape["dp"], mesh.shape["expert"]
    y_size = groups // 2
    x_size = y_size if lanes % y_size == 0 else 1
    fine = Mesh(mesh.devices.reshape(y_size, 2, lanes // x_size, x_size), ("y", "core", "z", "x"))
    split = ("y", "core", "z", "x")
    flat, deep = P(split, None), P(split, None, None)
    return jax.shard_map(
        local, mesh=fine, in_specs=(flat, flat, flat, deep, deep, deep), out_specs=flat, check_vma=False
    )
```

```python
from functools import partial

import jax
import jax.numpy as jnp
from jax import lax
from jax.experimental import pallas as pl
from jax.experimental.pallas import tpu as pltpu
from jax.sharding import Mesh, PartitionSpec as P

F32 = jnp.float32
BF16 = jnp.bfloat16
EXTRA = 128
MIB = 2**20


def divisor(size, most):
    return next(d for d in range(min(size, most), 0, -1) if size % d == 0)


def experts_kernel(
    info, x_hbm, g0, u0, d0, g1, u1, d1, o_hbm, x_ref, bg0, bu0, bd0, bg1, bu1, bd1, gate_ref, hid, o_ref, sems, out_sems,
    *, rows, top, tile, span
):
    total, width = o_ref.shape
    ff = g0.shape[1]
    spans = width // span
    x_copy = pltpu.make_async_copy(x_hbm, x_ref, sems.at[0])
    x_copy.start()
    ins = [pltpu.make_async_copy(src, dst, sems.at[1 + n]) for n, (src, dst) in enumerate(((g0, bg0), (u0, bu0), (g1, bg1), (u1, bu1)))]
    for c in ins:
        c.start()
    downs = []
    for n in range(spans):
        s = pl.ds(n * span, span)
        for m, (src, dst) in enumerate(((d0, bd0), (d1, bd1))):
            downs.append(pltpu.make_async_copy(src.at[:, s], dst.at[:, s], sems.at[5 + 2 * n + m]))
            downs[-1].start()
    x_copy.wait()

    ids = x_ref[:, width:].astype(F32)
    is_id = lax.broadcasted_iota(jnp.int32, ids.shape, 1) < top
    low, high, flip = info[0].astype(F32), info[1].astype(F32), info[2].astype(F32)
    has_low = jnp.max(jnp.where(is_id & (ids == low), 1.0, 0.0), axis=1, keepdims=True)
    has_high = jnp.max(jnp.where(is_id & (ids == high), 1.0, 0.0), axis=1, keepdims=True)
    share = jnp.broadcast_to(has_low * (1.0 - 0.5 * has_high), (total, 128)).astype(BF16)
    r = lax.broadcasted_iota(jnp.int32, (total, total), 0)
    c = lax.broadcasted_iota(jnp.int32, (total, total), 1)
    same = jnp.where(r // rows == c // rows, 1.0, 0.0).astype(BF16)
    low_rows = jnp.dot(same, share, preferred_element_type=F32)
    at = (lax.broadcasted_iota(jnp.int32, (total, 128), 0) % rows).astype(F32)
    is_low = jnp.where(at < low_rows, 1.0, 0.0)
    first = (is_low * (1.0 - flip) + (1.0 - is_low) * flip)[:, :1]

    for which, (bg, bu) in enumerate(((bg0, bu0), (bg1, bu1))):
        keep = first if which == 0 else 1.0 - first
        ins[2 * which].wait()

        @pl.loop(0, ff // tile)
        def _(t):
            s = pl.ds(pl.multiple_of(t * tile, tile), tile)
            gate_ref[:, s] = jnp.dot(x_ref[:, :width], bg[:, s], preferred_element_type=F32)

        ins[2 * which + 1].wait()

        @pl.loop(0, ff // tile)
        def _(t):
            s = pl.ds(pl.multiple_of(t * tile, tile), tile)
            up = jnp.dot(x_ref[:, :width], bu[:, s], preferred_element_type=F32)
            gate = gate_ref[:, s]
            h = jnp.where(keep > 0.5, gate / (1.0 + jnp.exp(-gate)) * up, 0.0)
            hid[:, pl.ds(pl.multiple_of(which * ff + t * tile, tile), tile)] = h.astype(BF16)

    outs = []
    for n in range(spans):
        downs[2 * n].wait()
        downs[2 * n + 1].wait()
        s = pl.ds(n * span, span)
        o_ref[:, s] = (
            jnp.dot(hid[:, :ff], bd0[:, s], preferred_element_type=F32)
            + jnp.dot(hid[:, ff:], bd1[:, s], preferred_element_type=F32)
        ).astype(BF16)
        outs.append(pltpu.make_async_copy(o_ref.at[:, s], o_hbm.at[:, s], out_sems.at[n]))
        outs[-1].start()
    for c in outs:
        c.wait()


def experts_apply(info, x, first, second, rows, top):
    width, ff = first[0].shape
    total = x.shape[0]
    span = divisor(width // 128, 8) * 128
    spans = width // span
    anywhere = pl.BlockSpec(memory_space=pl.ANY)
    return pl.pallas_call(
        partial(experts_kernel, rows=rows, top=top, tile=divisor(ff // 128, 2) * 128, span=span),
        out_shape=jax.ShapeDtypeStruct((total, width), BF16),
        grid_spec=pltpu.PrefetchScalarGridSpec(
            num_scalar_prefetch=1,
            grid=(1,),
            in_specs=[anywhere] * 7,
            out_specs=anywhere,
            scratch_shapes=[pltpu.VMEM(x.shape, BF16)]
            + [pltpu.VMEM(w.shape, BF16) for w in first + second]
            + [pltpu.VMEM((total, ff), F32), pltpu.VMEM((total, 2 * ff), BF16), pltpu.VMEM((total, width), BF16)]
            + [pltpu.SemaphoreType.DMA((5 + 2 * spans,)), pltpu.SemaphoreType.DMA((spans,))],
        ),
        compiler_params=pltpu.CompilerParams(vmem_limit_bytes=54 * MIB),
        cost_estimate=pl.CostEstimate(
            flops=12 * total * width * ff, bytes_accessed=12 * width * ff + 4 * total * width, transcendentals=2 * total * ff
        ),
    )(info, x, *first, *second)


def places(ids, plane_ids):
    chosen = jnp.any(ids[:, :, None, None] == plane_ids[None, None], axis=1)
    ones = chosen.astype(F32)
    tokens = ids.shape[0]
    before = (jnp.arange(tokens)[:, None] > jnp.arange(tokens)[None, :]).astype(F32)
    rank = jnp.einsum("ts,sjc->tjc", before, ones, preferred_element_type=F32)
    low_count = jnp.sum(ones[:, :, 0], axis=0)
    rank = rank + jnp.stack([jnp.zeros_like(low_count), low_count], axis=-1)[None]
    return jnp.where(chosen, rank, -1.0)


def after(value, *others):
    return lax.optimization_barrier((value,) + others)[0]


def local(tokens, router_weights, expert_ids, gate_weight, up_weight, down_weight):
    z_size = lax.axis_size("z")
    x_size = lax.axis_size("x")
    y_size = lax.axis_size("y")
    lane_count = z_size * x_size
    chips = y_size * x_size
    count, width = tokens.shape
    top = expert_ids.shape[1]
    rows = count * top // (y_size * lane_count)
    z_at = lax.axis_index("z")

    chip = jnp.arange(chips, dtype=jnp.int32)
    low = 2 * (chip // x_size) * lane_count + z_at * x_size + chip % x_size
    plane_ids = jnp.stack([low, low + lane_count], axis=-1).astype(F32)
    low_here = 2 * lax.axis_index("y") * lane_count + z_at * x_size + lax.axis_index("x")
    info = jnp.stack([low_here, low_here + lane_count, lax.axis_index("core")]).astype(jnp.int32)

    def flip(value, mask):
        return lax.ppermute(value, "z", [(i, i ^ mask) for i in range(z_size)])

    def inner(value):
        return lax.ppermute(value, "z", [(1, 2), (2, 1)])

    def outward(value):
        return lax.ppermute(value, "z", [(1, 0), (2, 3)])

    def inward(value):
        return lax.ppermute(value, "z", [(0, 1), (3, 2)])

    is_end = (z_at == 0) | (z_at == z_size - 1)

    hi = router_weights.astype(BF16)
    mid = (router_weights - hi.astype(F32)).astype(BF16)
    block = jnp.concatenate(
        [tokens, expert_ids.astype(BF16), hi, mid, jnp.zeros((count, EXTRA - 3 * top), BF16)], axis=1
    )

    swap = [(0, 1), (1, 0)]
    own = [gate_weight[0], up_weight[0], down_weight[0]]
    other = [lax.ppermute(w, "core", swap) for w in own]

    row = jnp.arange(rows, dtype=jnp.int32).astype(F32)

    def routed(part):
        extra = part[:, width:].astype(F32)
        rank = places(extra[:, :top], plane_ids)
        hit = rank[:, :, :, None] == row
        taken = jnp.any(hit, axis=2).reshape(count, chips * rows).astype(BF16)
        same = extra[:, :top, None, None] == plane_ids[None, None]
        mixes = []
        for n in (1, 2):
            w_of = jnp.sum(jnp.where(same, extra[:, n * top : (n + 1) * top, None, None], 0.0), axis=1)
            mixes.append(jnp.sum(jnp.where(hit, w_of[..., None], 0.0), axis=2).reshape(count, chips * rows).astype(BF16))
        return taken, mixes

    def exchange(value):
        moved = lax.all_to_all(value.reshape(chips, rows, value.shape[1]), ("y", "x"), 0, 0, tiled=True)
        return moved.reshape(value.shape)

    def gather(part, taken):
        return lax.dot_general(taken, part, (((0,), (0,)), ((), ())), preferred_element_type=F32).astype(BF16)

    def run(k, *others):
        outs[k] = experts_apply(info, after(arrived[k], *others), own, other, rows, top)

    line = z_size == 4
    moving = {k: flip(block, k) for k in ((1,) if line else range(1, z_size)) if k & (k - 1) == 0}
    if line:
        middle = inner(block)
    held, mixes, sent, arrived, outs = {0: block}, {}, {}, {}, {}
    for k in range(z_size):
        if k and line:
            if k == 1:
                held[1] = after(moving[1], sent[0])
                next_inner, next_outer = inner(held[1]), outward(after(middle, sent[0]))
            elif k == 2:
                passed = after(next_inner, sent[1])
                last_outer = outward(passed)
                held[2] = jnp.where(is_end, next_outer, passed)
            else:
                held[3] = jnp.where(is_end, after(last_outer, outs[0]), middle)
        elif k:
            bit = k & -k
            held[k] = after(moving[k] if k == bit else flip(held[k ^ bit], bit), sent[k - 1])
        taken, mixes[k] = routed(held[k])
        sent[k] = gather(held[k], taken)
        if k:
            sent[k] = after(sent[k], arrived[k - 1])
        if k > 1:
            run(k - 2, sent[k])
        arrived[k] = exchange(sent[k])
    last = z_size - 1
    run(last, *[outs[o] for o in outs])
    def mixed(k, arrived_back):
        return sum(jnp.dot(mix, arrived_back, preferred_element_type=F32) for mix in mixes[k])

    back, hold, extra = None, [], []
    for k in range(last, -1, -1):
        source = outs[k] if k == last else after(outs[k], back, *hold)
        if k < last:
            total, done = mixed(k + 1, after(back, source)), k + 1
            if not line:
                bit = done & -done
                total = sum((r for o, r in extra if o == done), total).astype(BF16)
                extra.append((done ^ bit, flip(total, bit).astype(F32)))
                hold = [total]
            elif done == 3:
                third = total
                hold = [total.astype(BF16)]
                from_end = inward(hold[0])
            elif done == 2:
                hold = [total.astype(BF16), (total + from_end.astype(F32)).astype(BF16)]
                near, far = inward(hold[0]), inner(hold[1])
            else:
                hold = [(total + far.astype(F32)).astype(BF16), (third + near.astype(F32)).astype(BF16)]
                extra += [(0, flip(hold[0], 1).astype(F32)), (0, inner(hold[1]).astype(F32))]
        if k and k - 1 not in outs:
            run(k - 1, source, *hold)
        back = exchange(source)
    return sum((r for o, r in extra if o == 0), mixed(0, back)).astype(BF16)


def solution(mesh):
    groups, lanes = mesh.shape["dp"], mesh.shape["expert"]
    y_size = groups // 2
    x_size = y_size if lanes % y_size == 0 else 1
    fine = Mesh(mesh.devices.reshape(y_size, 2, lanes // x_size, x_size), ("y", "core", "z", "x"))
    split = ("y", "core", "z", "x")
    flat, deep = P(split, None), P(split, None, None)
    return jax.shard_map(
        local, mesh=fine, in_specs=(flat, flat, flat, deep, deep, deep), out_specs=flat, check_vma=False
    )
```

```python
from functools import partial

import jax
import jax.numpy as jnp
from jax import lax
from jax.experimental import pallas as pl
from jax.experimental.pallas import tpu as pltpu
from jax.sharding import Mesh, PartitionSpec as P

F32 = jnp.float32
BF16 = jnp.bfloat16
EXTRA = 128
MIB = 2**20
ROUTE_COST = 400
MIX_COST = 4


def divisor(size, most):
    return next(d for d in range(min(size, most), 0, -1) if size % d == 0)


def experts_kernel(info, *refs, parts, rows, top, tile, span):
    x_hbm, refs = refs[:parts], refs[parts:]
    (g0, u0, d0, g1, u1, d1), refs = refs[:6], refs[6:]
    o_hbm, refs = refs[:parts], refs[parts:]
    x_ref, bg0, bu0, bd0, bg1, bu1, bd1, gate_ref, hid, o_ref, sems, out_sems = refs
    total, width = o_ref.shape
    ff = g0.shape[1]
    spans = width // span
    held = [pl.ds(p * (total // parts), total // parts) for p in range(parts)]
    x_copies = [pltpu.make_async_copy(x_hbm[p], x_ref.at[held[p]], sems.at[4 + 2 * spans + p]) for p in range(parts)]
    for c in x_copies:
        c.start()
    ins = [pltpu.make_async_copy(src, dst, sems.at[n]) for n, (src, dst) in enumerate(((g0, bg0), (u0, bu0), (g1, bg1), (u1, bu1)))]
    for c in ins:
        c.start()
    downs = []
    for n in range(spans):
        s = pl.ds(n * span, span)
        for m, (src, dst) in enumerate(((d0, bd0), (d1, bd1))):
            downs.append(pltpu.make_async_copy(src.at[:, s], dst.at[:, s], sems.at[4 + 2 * n + m]))
            downs[-1].start()
    for c in x_copies:
        c.wait()

    ids = x_ref[:, width:].astype(F32)
    is_id = lax.broadcasted_iota(jnp.int32, ids.shape, 1) < top
    low, high, flip = info[0].astype(F32), info[1].astype(F32), info[2].astype(F32)
    has_low = jnp.max(jnp.where(is_id & (ids == low), 1.0, 0.0), axis=1, keepdims=True)
    has_high = jnp.max(jnp.where(is_id & (ids == high), 1.0, 0.0), axis=1, keepdims=True)
    share = jnp.broadcast_to(has_low * (1.0 - 0.5 * has_high), (total, 128)).astype(BF16)
    r = lax.broadcasted_iota(jnp.int32, (total, total), 0)
    c = lax.broadcasted_iota(jnp.int32, (total, total), 1)
    same = jnp.where(r // rows == c // rows, 1.0, 0.0).astype(BF16)
    low_rows = jnp.dot(same, share, preferred_element_type=F32)
    at = (lax.broadcasted_iota(jnp.int32, (total, 128), 0) % rows).astype(F32)
    is_low = jnp.where(at < low_rows, 1.0, 0.0)
    first = (is_low * (1.0 - flip) + (1.0 - is_low) * flip)[:, :1]

    for which, (bg, bu) in enumerate(((bg0, bu0), (bg1, bu1))):
        keep = first if which == 0 else 1.0 - first
        ins[2 * which].wait()

        @pl.loop(0, ff // tile)
        def _(t):
            s = pl.ds(pl.multiple_of(t * tile, tile), tile)
            gate_ref[:, s] = jnp.dot(x_ref[:, :width], bg[:, s], preferred_element_type=F32)

        ins[2 * which + 1].wait()

        @pl.loop(0, ff // tile)
        def _(t):
            s = pl.ds(pl.multiple_of(t * tile, tile), tile)
            up = jnp.dot(x_ref[:, :width], bu[:, s], preferred_element_type=F32)
            gate = gate_ref[:, s]
            h = jnp.where(keep > 0.5, gate / (1.0 + jnp.exp(-gate)) * up, 0.0)
            hid[:, pl.ds(pl.multiple_of(which * ff + t * tile, tile), tile)] = h.astype(BF16)

    outs = []
    for n in range(spans):
        downs[2 * n].wait()
        downs[2 * n + 1].wait()
        s = pl.ds(n * span, span)
        o_ref[:, s] = (
            jnp.dot(hid[:, :ff], bd0[:, s], preferred_element_type=F32)
            + jnp.dot(hid[:, ff:], bd1[:, s], preferred_element_type=F32)
        ).astype(BF16)
        for p in range(parts):
            outs.append(pltpu.make_async_copy(o_ref.at[held[p], s], o_hbm[p].at[:, s], out_sems.at[n, p]))
            outs[-1].start()
    for c in outs:
        c.wait()


def experts_apply(info, xs, first, second, rows, top):
    width, ff = first[0].shape
    parts, each = len(xs), xs[0].shape[0]
    total = parts * each
    span = divisor(width // 128, 8) * 128
    spans = width // span
    anywhere = pl.BlockSpec(memory_space=pl.ANY)
    return pl.pallas_call(
        partial(experts_kernel, parts=parts, rows=rows, top=top, tile=divisor(ff // 128, 2) * 128, span=span),
        out_shape=[jax.ShapeDtypeStruct((each, width), BF16)] * parts,
        grid_spec=pltpu.PrefetchScalarGridSpec(
            num_scalar_prefetch=1,
            grid=(1,),
            in_specs=[anywhere] * (parts + 6),
            out_specs=[anywhere] * parts,
            scratch_shapes=[pltpu.VMEM((total, xs[0].shape[1]), BF16)]
            + [pltpu.VMEM(w.shape, BF16) for w in first + second]
            + [pltpu.VMEM((total, ff), F32), pltpu.VMEM((total, 2 * ff), BF16), pltpu.VMEM((total, width), BF16)]
            + [pltpu.SemaphoreType.DMA((4 + 2 * spans + parts,)), pltpu.SemaphoreType.DMA((spans, parts))],
        ),
        compiler_params=pltpu.CompilerParams(vmem_limit_bytes=54 * MIB),
        cost_estimate=pl.CostEstimate(
            flops=12 * total * width * ff, bytes_accessed=12 * width * ff + 4 * total * width, transcendentals=2 * total * ff
        ),
    )(info, *xs, *first, *second)


def pack_kernel(tokens, ids, weights, out):
    count, width = tokens.shape
    top = ids.shape[1]
    out[:, :width] = tokens[...]
    hi = weights[...].astype(BF16)
    mid = (weights[...] - hi.astype(F32)).astype(BF16)
    rest = jnp.zeros((count, EXTRA - 3 * top), F32)
    extra = [ids[...].astype(F32), hi.astype(F32), mid.astype(F32), rest]
    out[:, width:] = jnp.concatenate(extra, axis=1).astype(BF16)


def pack(tokens, ids, weights):
    count, width = tokens.shape
    return pl.pallas_call(
        pack_kernel,
        out_shape=jax.ShapeDtypeStruct((count, width + EXTRA), BF16),
        compiler_params=pltpu.CompilerParams(vmem_limit_bytes=16 * MIB),
    )(tokens, ids, weights)


def route_kernel(flag, plane, *refs, choices, parts, rows, top, width):
    blocks, outs, (mix_hi, mix_mid) = refs[:choices], refs[choices : choices + parts], refs[choices + parts :]

    def block(s):
        value = blocks[0][:, s]
        return value if choices == 1 else jnp.where(flag[0] != 0, value, blocks[1][:, s])

    extra = block(slice(width, width + EXTRA)).astype(F32)
    count = extra.shape[0]
    lanes = mix_hi.shape[1]
    ids = plane[:1, :]
    chosen = jnp.zeros((count, 128), F32)
    w_hi, w_mid = chosen, chosen
    for k in range(top):
        same = extra[:, k : k + 1] == ids
        chosen = jnp.where(same, 1.0, chosen)
        w_hi = jnp.where(same, extra[:, top + k : top + k + 1], w_hi)
        w_mid = jnp.where(same, extra[:, 2 * top + k : 2 * top + k + 1], w_mid)

    def table(shape, test):
        r = lax.broadcasted_iota(jnp.int32, shape, 0)
        c = lax.broadcasted_iota(jnp.int32, shape, 1)
        return jnp.where(test(r, c), 1.0, 0.0).astype(BF16)

    def dot(a, b):
        return jnp.dot(a.astype(BF16), b.astype(BF16), preferred_element_type=F32)

    before = table((count, count), lambda r, c: c < r)
    to_high = table((128, 128), lambda r, c: (c == r + 1) & (r % 2 == 0))
    rank = dot(before, chosen) + dot(jnp.ones((count, count), F32), dot(chosen, to_high))
    rank = jnp.where(chosen > 0.0, rank, -1.0)
    at = (lax.broadcasted_iota(jnp.int32, (count, lanes), 1) % rows).astype(F32)
    taken = jnp.zeros((count, lanes), F32)
    sum_hi, sum_mid = taken, taken
    for side in range(2):
        spread = table((128, lanes), lambda r, c: r == 2 * (c // rows) + side)
        hit = dot(rank, spread) == at
        taken = jnp.where(hit, 1.0, taken)
        sum_hi = jnp.where(hit, dot(w_hi, spread), sum_hi)
        sum_mid = jnp.where(hit, dot(w_mid, spread), sum_mid)
    mix_hi[...] = sum_hi.astype(BF16)
    mix_mid[...] = sum_mid.astype(BF16)
    taken = taken.astype(BF16)
    step = divisor((width + EXTRA) // 128, 11) * 128
    each = lanes // parts
    for n in range((width + EXTRA) // step):
        s = slice(n * step, (n + 1) * step)
        got = lax.dot_general(taken, block(s), (((0,), (0,)), ((), ())), preferred_element_type=F32).astype(BF16)
        for p in range(parts):
            outs[p][:, s] = got[p * each : (p + 1) * each]


def route(flag, plane, blocks, parts, rows, top):
    count, wide = blocks[0].shape
    lanes = parts * rows if parts > 1 else plane.shape[0] * rows
    each = lanes // parts
    chips = lanes // rows
    ids = jnp.full((8, 128), -1.0, F32).at[:, : 2 * chips].set(plane.reshape(1, -1))
    whole = pl.BlockSpec(memory_space=pltpu.VMEM)
    out = pl.pallas_call(
        partial(route_kernel, choices=len(blocks), parts=parts, rows=rows, top=top, width=wide - EXTRA),
        in_specs=[pl.BlockSpec(memory_space=pltpu.SMEM), whole] + [whole] * len(blocks),
        out_specs=[whole] * (parts + 2),
        out_shape=[jax.ShapeDtypeStruct((each, wide), BF16)] * parts + [jax.ShapeDtypeStruct((count, lanes), BF16)] * 2,
        compiler_params=pltpu.CompilerParams(vmem_limit_bytes=24 * MIB),
        cost_estimate=pl.CostEstimate(flops=ROUTE_COST * count * lanes * wide, bytes_accessed=2 * (count + lanes) * wide, transcendentals=0),
    )(flag, ids, *blocks)
    return out[:parts], out[parts:]


def mix_kernel(hi, mid, *refs, parts, terms):
    backs, refs = refs[:parts], refs[parts:]
    adds, outs = refs[: len(refs) - len(terms)], refs[len(refs) - len(terms) :]
    rows = jnp.concatenate([b[...] for b in backs], axis=0)
    total = jnp.dot(hi[...], rows, preferred_element_type=F32) + jnp.dot(mid[...], rows, preferred_element_type=F32)
    for (with_total, used), out in zip(terms, outs):
        value = total if with_total else None
        for n in used:
            add = adds[n][...].astype(F32)
            value = add if value is None else value + add
        out[...] = value.astype(out.dtype)


def mix_rows(mix, backs, adds, terms, dtypes):
    count, lanes = mix[0].shape
    width = backs[0].shape[1]
    step = divisor(width // 128, 8) * 128
    full = pl.BlockSpec((count, lanes), lambda n: (0, 0))
    tall = pl.BlockSpec((count, step), lambda n: (0, n))
    return pl.pallas_call(
        partial(mix_kernel, parts=len(backs), terms=tuple(terms)),
        grid=(width // step,),
        in_specs=[full, full] + [pl.BlockSpec((b.shape[0], step), lambda n: (0, n)) for b in backs] + [tall] * len(adds),
        out_specs=[tall] * len(terms),
        out_shape=[jax.ShapeDtypeStruct((count, width), d) for d in dtypes],
        compiler_params=pltpu.CompilerParams(vmem_limit_bytes=24 * MIB),
        cost_estimate=pl.CostEstimate(flops=MIX_COST * count * lanes * width, bytes_accessed=6 * count * width, transcendentals=0),
    )(*mix, *backs, *adds)


def after(value, *others):
    return lax.optimization_barrier((value,) + others)[0]


def local(tokens, router_weights, expert_ids, gate_weight, up_weight, down_weight):
    z_size = lax.axis_size("z")
    x_size = lax.axis_size("x")
    y_size = lax.axis_size("y")
    lane_count = z_size * x_size
    chips = y_size * x_size
    count, width = tokens.shape
    top = expert_ids.shape[1]
    rows = count * top // (y_size * lane_count)
    z_at = lax.axis_index("z")

    parts = 1
    here = lax.axis_index("y") * x_size + lax.axis_index("x")
    chip = jnp.arange(chips, dtype=jnp.int32)
    chip = chip ^ here if parts > 1 else chip
    low = 2 * (chip // x_size) * lane_count + z_at * x_size + chip % x_size
    plane = jnp.stack([low, low + lane_count], axis=-1).astype(F32)
    low_here = 2 * lax.axis_index("y") * lane_count + z_at * x_size + lax.axis_index("x")
    info = jnp.stack([low_here, low_here + lane_count, lax.axis_index("core")]).astype(jnp.int32)

    def flip(value, mask):
        return lax.ppermute(value, "z", [(i, i ^ mask) for i in range(z_size)])

    def inner(value):
        return lax.ppermute(value, "z", [(1, 2), (2, 1)])

    def outward(value):
        return lax.ppermute(value, "z", [(1, 0), (2, 3)])

    def inward(value):
        return lax.ppermute(value, "z", [(0, 1), (3, 2)])

    is_end = (z_at == 0) | (z_at == z_size - 1)

    block = pack(tokens, expert_ids, router_weights)
    flag = is_end.astype(jnp.int32).reshape(1)
    swap = [(0, 1), (1, 0)]
    own = [gate_weight[0], up_weight[0], down_weight[0]]
    other = [lax.ppermute(w, "core", swap) for w in own]

    def exchange(values):
        if parts == 1:
            value = values[0].reshape(chips, rows, values[0].shape[1])
            return [lax.all_to_all(value, ("y", "x"), 0, 0, tiled=True).reshape(values[0].shape)]
        pairs = [[(i, i ^ m) for i in range(chips)] for m in range(chips)]
        return [values[0]] + [lax.ppermute(values[m], ("y", "x"), pairs[m]) for m in range(1, chips)]

    def run(k, *others):
        outs[k] = experts_apply(info, after(arrived[k], *others), own, other, rows, top)

    line = z_size == 4
    moving = {k: flip(block, k) for k in ((1,) if line else range(1, z_size)) if k & (k - 1) == 0}
    if line:
        middle = inner(block)
    held, mixes, sent, arrived, outs = {0: [block]}, {}, {}, {}, {}
    for k in range(z_size):
        if k and line:
            if k == 1:
                held[1] = [after(moving[1], sent[0])]
                next_inner, next_outer = inner(held[1][0]), outward(after(middle, sent[0]))
            elif k == 2:
                passed = after(next_inner, sent[1])
                last_outer = outward(passed)
                held[2] = [next_outer, passed]
            else:
                held[3] = [after(last_outer, outs[0]), middle]
        elif k:
            bit = k & -k
            held[k] = [after(moving[k] if k == bit else flip(held[k ^ bit][0], bit), sent[k - 1])]
        sent[k], mixes[k] = route(flag, plane, held[k], parts, rows, top)
        if k and parts == 1:
            sent[k] = after(sent[k], arrived[k - 1])
        if k > 1:
            run(k - 2, sent[k])
        arrived[k] = exchange(sent[k])
    last = z_size - 1
    run(last, *[outs[o] for o in outs])

    back, hold, extra = None, [], []
    for k in range(last, -1, -1):
        source = outs[k] if k == last else after(outs[k], *hold, *(back if parts == 1 else []))
        if k < last:
            done = k + 1
            got = after(back, source)
            if not line:
                bit = done & -done
                adds = [r for o, r in extra if o == done]
                hold = mix_rows(mixes[done], got, adds, [(True, range(len(adds)))], [BF16])
                extra.append((done ^ bit, flip(hold[0], bit)))
            elif done == 3:
                third, total = mix_rows(mixes[3], got, [], [(True, ()), (True, ())], [F32, BF16])
                hold = [total]
                from_end = inward(total)
            elif done == 2:
                hold = mix_rows(mixes[2], got, [from_end], [(True, ()), (True, (0,))], [BF16] * 2)
                near, far = inward(hold[0]), inner(hold[1])
            else:
                hold = mix_rows(mixes[1], got, [far, third, near], [(True, (0,)), (False, (1, 2))], [BF16] * 2)
                extra += [(0, flip(hold[0], 1)), (0, inner(hold[1]))]
        if k and k - 1 not in outs:
            run(k - 1, source, *hold)
        back = exchange(source)
    adds = [r for o, r in extra if o == 0]
    return mix_rows(mixes[0], back, adds, [(True, range(len(adds)))], [BF16])[0]


def solution(mesh):
    groups, lanes = mesh.shape["dp"], mesh.shape["expert"]
    y_size = groups // 2
    x_size = y_size if lanes % y_size == 0 else 1
    fine = Mesh(mesh.devices.reshape(y_size, 2, lanes // x_size, x_size), ("y", "core", "z", "x"))
    split = ("y", "core", "z", "x")
    flat, deep = P(split, None), P(split, None, None)
    return jax.shard_map(
        local, mesh=fine, in_specs=(flat, flat, flat, deep, deep, deep), out_specs=flat, check_vma=False
    )
```

```python
from functools import partial

import jax
import jax.numpy as jnp
from jax import lax
from jax.experimental import pallas as pl
from jax.experimental.pallas import tpu as pltpu
from jax.sharding import Mesh, PartitionSpec as P

F32 = jnp.float32
BF16 = jnp.bfloat16
EXTRA = 128
MIB = 2**20
PERMUTED = (2, 3)
ROUTE_COST = 400
MIX_COST = 4


def divisor(size, most):
    return next(d for d in range(min(size, most), 0, -1) if size % d == 0)


def experts_kernel(info, *refs, given, parts, rows, top, tile, span):
    x_hbm, refs = refs[:given], refs[given:]
    (g0, u0, d0, g1, u1, d1), refs = refs[:6], refs[6:]
    o_hbm, refs = refs[:parts], refs[parts:]
    x_ref, bg0, bu0, bd0, bg1, bu1, bd1, gate_ref, hid, o_ref, sems, out_sems = refs
    total, width = o_ref.shape
    ff = g0.shape[1]
    spans = width // span
    each = total // parts
    held = [pl.ds(pl.multiple_of((info[3] ^ p) * each, each), each) if parts > 1 else pl.ds(0, total) for p in range(parts)]
    if given == 1:
        x_copies = [pltpu.make_async_copy(x_hbm[0], x_ref, sems.at[4 + 2 * spans])]
    else:
        x_copies = [pltpu.make_async_copy(x_hbm[p], x_ref.at[held[p]], sems.at[4 + 2 * spans + p]) for p in range(parts)]
    for c in x_copies:
        c.start()
    ins = [pltpu.make_async_copy(src, dst, sems.at[n]) for n, (src, dst) in enumerate(((g0, bg0), (u0, bu0), (g1, bg1), (u1, bu1)))]
    for c in ins:
        c.start()
    downs = []
    for n in range(spans):
        s = pl.ds(n * span, span)
        for m, (src, dst) in enumerate(((d0, bd0), (d1, bd1))):
            downs.append(pltpu.make_async_copy(src.at[:, s], dst.at[:, s], sems.at[4 + 2 * n + m]))
            downs[-1].start()
    for c in x_copies:
        c.wait()

    ids = x_ref[:, width:].astype(F32)
    is_id = lax.broadcasted_iota(jnp.int32, ids.shape, 1) < top
    low, high, flip = info[0].astype(F32), info[1].astype(F32), info[2].astype(F32)
    has_low = jnp.max(jnp.where(is_id & (ids == low), 1.0, 0.0), axis=1, keepdims=True)
    has_high = jnp.max(jnp.where(is_id & (ids == high), 1.0, 0.0), axis=1, keepdims=True)
    share = jnp.broadcast_to(has_low * (1.0 - 0.5 * has_high), (total, 128)).astype(BF16)
    r = lax.broadcasted_iota(jnp.int32, (total, total), 0)
    c = lax.broadcasted_iota(jnp.int32, (total, total), 1)
    same = jnp.where(r // rows == c // rows, 1.0, 0.0).astype(BF16)
    low_rows = jnp.dot(same, share, preferred_element_type=F32)
    at = (lax.broadcasted_iota(jnp.int32, (total, 128), 0) % rows).astype(F32)
    is_low = jnp.where(at < low_rows, 1.0, 0.0)
    first = (is_low * (1.0 - flip) + (1.0 - is_low) * flip)[:, :1]

    for which, (bg, bu) in enumerate(((bg0, bu0), (bg1, bu1))):
        keep = first if which == 0 else 1.0 - first
        ins[2 * which].wait()

        @pl.loop(0, ff // tile)
        def _(t):
            s = pl.ds(pl.multiple_of(t * tile, tile), tile)
            gate_ref[:, s] = jnp.dot(x_ref[:, :width], bg[:, s], preferred_element_type=F32)

        ins[2 * which + 1].wait()

        @pl.loop(0, ff // tile)
        def _(t):
            s = pl.ds(pl.multiple_of(t * tile, tile), tile)
            up = jnp.dot(x_ref[:, :width], bu[:, s], preferred_element_type=F32)
            gate = gate_ref[:, s]
            h = jnp.where(keep > 0.5, gate / (1.0 + jnp.exp(-gate)) * up, 0.0)
            hid[:, pl.ds(pl.multiple_of(which * ff + t * tile, tile), tile)] = h.astype(BF16)

    outs = []
    for n in range(spans):
        downs[2 * n].wait()
        downs[2 * n + 1].wait()
        s = pl.ds(n * span, span)
        o_ref[:, s] = (
            jnp.dot(hid[:, :ff], bd0[:, s], preferred_element_type=F32)
            + jnp.dot(hid[:, ff:], bd1[:, s], preferred_element_type=F32)
        ).astype(BF16)
        for p in range(parts):
            outs.append(pltpu.make_async_copy(o_ref.at[held[p], s], o_hbm[p].at[:, s], out_sems.at[n, p]))
            outs[-1].start()
    for c in outs:
        c.wait()


def experts_apply(info, xs, first, second, parts, rows, top):
    width, ff = first[0].shape
    given = len(xs)
    total = given * xs[0].shape[0]
    each = total // parts
    span = divisor(width // 128, 8) * 128
    spans = width // span
    anywhere = pl.BlockSpec(memory_space=pl.ANY)
    return pl.pallas_call(
        partial(experts_kernel, given=given, parts=parts, rows=rows, top=top, tile=divisor(ff // 128, 2) * 128, span=span),
        out_shape=[jax.ShapeDtypeStruct((each, width), BF16)] * parts,
        grid_spec=pltpu.PrefetchScalarGridSpec(
            num_scalar_prefetch=1,
            grid=(1,),
            in_specs=[anywhere] * (given + 6),
            out_specs=[anywhere] * parts,
            scratch_shapes=[pltpu.VMEM((total, xs[0].shape[1]), BF16)]
            + [pltpu.VMEM(w.shape, BF16) for w in first + second]
            + [pltpu.VMEM((total, ff), F32), pltpu.VMEM((total, 2 * ff), BF16), pltpu.VMEM((total, width), BF16)]
            + [pltpu.SemaphoreType.DMA((4 + 2 * spans + given,)), pltpu.SemaphoreType.DMA((spans, parts))],
        ),
        compiler_params=pltpu.CompilerParams(vmem_limit_bytes=54 * MIB),
        cost_estimate=pl.CostEstimate(
            flops=12 * total * width * ff, bytes_accessed=12 * width * ff + 4 * total * width, transcendentals=2 * total * ff
        ),
    )(info, *xs, *first, *second)


def pack_kernel(tokens, ids, weights, out):
    count, width = tokens.shape
    top = ids.shape[1]
    out[:, :width] = tokens[...]
    hi = weights[...].astype(BF16)
    mid = (weights[...] - hi.astype(F32)).astype(BF16)
    rest = jnp.zeros((count, EXTRA - 3 * top), F32)
    extra = [ids[...].astype(F32), hi.astype(F32), mid.astype(F32), rest]
    out[:, width:] = jnp.concatenate(extra, axis=1).astype(BF16)


def pack(tokens, ids, weights):
    count, width = tokens.shape
    return pl.pallas_call(
        pack_kernel,
        out_shape=jax.ShapeDtypeStruct((count, width + EXTRA), BF16),
        compiler_params=pltpu.CompilerParams(vmem_limit_bytes=16 * MIB),
    )(tokens, ids, weights)


def route_kernel(flag, plane, *refs, choices, sends, relative, rows, top, width):
    blocks, outs, (mix_hi, mix_mid) = refs[:choices], refs[choices : choices + sends], refs[choices + sends :]

    def block(s):
        value = blocks[0][:, s]
        return value if choices == 1 else jnp.where(flag[0] != 0, value, blocks[1][:, s])

    extra = block(slice(width, width + EXTRA)).astype(F32)
    count = extra.shape[0]
    lanes = mix_hi.shape[1]
    ids = plane[:1, :]
    chosen = jnp.zeros((count, 128), F32)
    w_hi, w_mid = chosen, chosen
    for k in range(top):
        same = extra[:, k : k + 1] == ids
        chosen = jnp.where(same, 1.0, chosen)
        w_hi = jnp.where(same, extra[:, top + k : top + k + 1], w_hi)
        w_mid = jnp.where(same, extra[:, 2 * top + k : 2 * top + k + 1], w_mid)

    def table(shape, test):
        r = lax.broadcasted_iota(jnp.int32, shape, 0)
        c = lax.broadcasted_iota(jnp.int32, shape, 1)
        return jnp.where(test(r, c), 1.0, 0.0).astype(BF16)

    def dot(a, b):
        return jnp.dot(a.astype(BF16), b.astype(BF16), preferred_element_type=F32)

    before = table((count, count), lambda r, c: c < r)
    to_high = table((128, 128), lambda r, c: (c == r + 1) & (r % 2 == 0))
    rank = dot(before, chosen) + dot(jnp.ones((count, count), F32), dot(chosen, to_high))
    rank = jnp.where(chosen > 0.0, rank, -1.0)
    at = (lax.broadcasted_iota(jnp.int32, (count, lanes), 1) % rows).astype(F32)
    taken = jnp.zeros((count, lanes), F32)
    sum_hi, sum_mid, taken_back = taken, taken, taken
    for side in range(2):
        spread = table((128, lanes), lambda r, c: r == 2 * (c // rows) + side)
        hit = dot(rank, spread) == at
        taken = jnp.where(hit, 1.0, taken)
        if relative:
            spread = table((128, lanes), lambda r, c: r == 2 * ((c // rows) ^ flag[1]) + side)
            hit = dot(rank, spread) == at
            if sends > 1:
                taken_back = jnp.where(hit, 1.0, taken_back)
        sum_hi = jnp.where(hit, dot(w_hi, spread), sum_hi)
        sum_mid = jnp.where(hit, dot(w_mid, spread), sum_mid)
    mix_hi[...] = sum_hi.astype(BF16)
    mix_mid[...] = sum_mid.astype(BF16)
    taken = (taken_back if sends > 1 else taken).astype(BF16)
    each = lanes // sends
    step = divisor((width + EXTRA) // 128, 11) * 128
    for n in range((width + EXTRA) // step):
        s = slice(n * step, (n + 1) * step)
        got = lax.dot_general(taken, block(s), (((0,), (0,)), ((), ())), preferred_element_type=F32).astype(BF16)
        for p in range(sends):
            outs[p][:, s] = got[p * each : (p + 1) * each]


def route(flag, plane, blocks, sends, relative, rows, top):
    count, wide = blocks[0].shape
    chips = plane.shape[0]
    lanes = chips * rows
    ids = jnp.full((8, 128), -1.0, F32).at[:, : 2 * chips].set(plane.reshape(1, -1))
    whole = pl.BlockSpec(memory_space=pltpu.VMEM)
    out = pl.pallas_call(
        partial(route_kernel, choices=len(blocks), sends=sends, relative=relative, rows=rows, top=top, width=wide - EXTRA),
        in_specs=[pl.BlockSpec(memory_space=pltpu.SMEM), whole] + [whole] * len(blocks),
        out_specs=[whole] * (sends + 2),
        out_shape=[jax.ShapeDtypeStruct((lanes // sends, wide), BF16)] * sends
        + [jax.ShapeDtypeStruct((count, lanes), BF16)] * 2,
        compiler_params=pltpu.CompilerParams(vmem_limit_bytes=24 * MIB),
        cost_estimate=pl.CostEstimate(flops=ROUTE_COST * count * lanes * wide, bytes_accessed=2 * (count + lanes) * wide, transcendentals=0),
    )(flag, ids, *blocks)
    return out[:sends], out[sends:]


def mix_kernel(hi, mid, *refs, parts, terms):
    backs, refs = refs[:parts], refs[parts:]
    adds, outs = refs[: len(refs) - len(terms)], refs[len(refs) - len(terms) :]
    rows = jnp.concatenate([b[...] for b in backs], axis=0)
    total = jnp.dot(hi[...], rows, preferred_element_type=F32) + jnp.dot(mid[...], rows, preferred_element_type=F32)
    for (with_total, used), out in zip(terms, outs):
        value = total if with_total else None
        for n in used:
            add = adds[n][...].astype(F32)
            value = add if value is None else value + add
        out[...] = value.astype(out.dtype)


def mix_rows(mix, backs, adds, terms, dtypes):
    count, lanes = mix[0].shape
    width = backs[0].shape[1]
    step = divisor(width // 128, 8) * 128
    full = pl.BlockSpec((count, lanes), lambda n: (0, 0))
    tall = pl.BlockSpec((count, step), lambda n: (0, n))
    return pl.pallas_call(
        partial(mix_kernel, parts=len(backs), terms=tuple(terms)),
        grid=(width // step,),
        in_specs=[full, full] + [pl.BlockSpec((b.shape[0], step), lambda n: (0, n)) for b in backs] + [tall] * len(adds),
        out_specs=[tall] * len(terms),
        out_shape=[jax.ShapeDtypeStruct((count, width), d) for d in dtypes],
        compiler_params=pltpu.CompilerParams(vmem_limit_bytes=24 * MIB),
        cost_estimate=pl.CostEstimate(flops=MIX_COST * count * lanes * width, bytes_accessed=6 * count * width, transcendentals=0),
    )(*mix, *backs, *adds)


def after(value, *others):
    return lax.optimization_barrier((value,) + others)[0]


def local(tokens, router_weights, expert_ids, gate_weight, up_weight, down_weight):
    z_size = lax.axis_size("z")
    x_size = lax.axis_size("x")
    y_size = lax.axis_size("y")
    lane_count = z_size * x_size
    chips = y_size * x_size
    count, width = tokens.shape
    top = expert_ids.shape[1]
    rows = count * top // (y_size * lane_count)
    z_at = lax.axis_index("z")

    parts = chips if chips in (2, 4) else 1
    here = lax.axis_index("y") * x_size + lax.axis_index("x")
    chip = jnp.arange(chips, dtype=jnp.int32)
    low = 2 * (chip // x_size) * lane_count + z_at * x_size + chip % x_size
    plane = jnp.stack([low, low + lane_count], axis=-1).astype(F32)
    low_here = 2 * lax.axis_index("y") * lane_count + z_at * x_size + lax.axis_index("x")
    info = jnp.stack([low_here, low_here + lane_count, lax.axis_index("core"), here]).astype(jnp.int32)

    def flip(value, mask):
        return lax.ppermute(value, "z", [(i, i ^ mask) for i in range(z_size)])

    def inner(value):
        return lax.ppermute(value, "z", [(1, 2), (2, 1)])

    def outward(value):
        return lax.ppermute(value, "z", [(1, 0), (2, 3)])

    def inward(value):
        return lax.ppermute(value, "z", [(0, 1), (3, 2)])

    is_end = (z_at == 0) | (z_at == z_size - 1)

    block = pack(tokens, expert_ids, router_weights)
    flag = jnp.stack([is_end.astype(jnp.int32), here])
    swap = [(0, 1), (1, 0)]
    own = [gate_weight[0], up_weight[0], down_weight[0]]
    other = [lax.ppermute(w, "core", swap) for w in own]

    def exchange(values):
        if len(values) == 1:
            value = values[0].reshape(chips, rows, values[0].shape[1])
            return [lax.all_to_all(value, ("y", "x"), 0, 0, tiled=True).reshape(values[0].shape)]
        pairs = [[(i, i ^ m) for i in range(chips)] for m in range(chips)]
        return [values[0]] + [lax.ppermute(values[m], ("y", "x"), pairs[m]) for m in range(1, chips)]

    def run(k, *others):
        outs[k] = experts_apply(info, after(arrived[k], *others), own, other, parts, rows, top)

    line = z_size == 4
    moving = {k: flip(block, k) for k in ((1,) if line else range(1, z_size)) if k & (k - 1) == 0}
    if line:
        middle = inner(block)
    held, mixes, sent, arrived, outs = {0: [block]}, {}, {}, {}, {}
    for k in range(z_size):
        if k and line:
            if k == 1:
                held[1] = [after(moving[1], sent[0])]
                next_inner, next_outer = inner(held[1][0]), outward(after(middle, sent[0]))
            elif k == 2:
                passed = after(next_inner, sent[1])
                last_outer = outward(passed)
                held[2] = [next_outer, passed]
            else:
                held[3] = [after(last_outer, outs[0]), middle]
        elif k:
            bit = k & -k
            held[k] = [after(moving[k] if k == bit else flip(held[k ^ bit][0], bit), sent[k - 1])]
        sends = parts if k in PERMUTED else 1
        sent[k], mixes[k] = route(flag, plane, held[k], sends, parts > 1, rows, top)
        if k and sends == 1:
            sent[k] = after(sent[k], arrived[k - 1])
        if k > 1:
            run(k - 2, sent[k])
        arrived[k] = exchange(sent[k])
    last = z_size - 1
    run(last, *[outs[o] for o in outs])

    back, hold, extra = None, [], []
    for k in range(last, -1, -1):
        source = outs[k] if k == last else after(outs[k], *hold, *(back if parts == 1 else []))
        if k < last:
            done = k + 1
            got = after(back, source)
            if not line:
                bit = done & -done
                adds = [r for o, r in extra if o == done]
                hold = mix_rows(mixes[done], got, adds, [(True, range(len(adds)))], [BF16])
                extra.append((done ^ bit, flip(hold[0], bit)))
            elif done == 3:
                third, total = mix_rows(mixes[3], got, [], [(True, ()), (True, ())], [F32, BF16])
                hold = [total]
                from_end = inward(total)
            elif done == 2:
                hold = mix_rows(mixes[2], got, [from_end], [(True, ()), (True, (0,))], [BF16] * 2)
                near, far = inward(hold[0]), inner(hold[1])
            else:
                hold = mix_rows(mixes[1], got, [far, third, near], [(True, (0,)), (False, (1, 2))], [BF16] * 2)
                extra += [(0, flip(hold[0], 1)), (0, inner(hold[1]))]
        if k and k - 1 not in outs:
            run(k - 1, source, *hold)
        back = exchange(source)
    adds = [r for o, r in extra if o == 0]
    return mix_rows(mixes[0], back, adds, [(True, range(len(adds)))], [BF16])[0]


def solution(mesh):
    groups, lanes = mesh.shape["dp"], mesh.shape["expert"]
    y_size = groups // 2
    x_size = y_size if lanes % y_size == 0 else 1
    fine = Mesh(mesh.devices.reshape(y_size, 2, lanes // x_size, x_size), ("y", "core", "z", "x"))
    split = ("y", "core", "z", "x")
    flat, deep = P(split, None), P(split, None, None)
    return jax.shard_map(
        local, mesh=fine, in_specs=(flat, flat, flat, deep, deep, deep), out_specs=flat, check_vma=False
    )
```

```python
from functools import partial

import jax
import jax.numpy as jnp
from jax import lax
from jax.experimental import pallas as pl
from jax.experimental.pallas import tpu as pltpu
from jax.sharding import Mesh, PartitionSpec as P

F32 = jnp.float32
BF16 = jnp.bfloat16
EXTRA = 128
MIB = 2**20
PERMUTED = (2, 3)
ROUTE_COST = 400
MIX_COST = 4


def divisor(size, most):
    return next(d for d in range(min(size, most), 0, -1) if size % d == 0)


def experts_kernel(info, *refs, given, parts, rows, top, tile, span):
    x_hbm, refs = refs[:given], refs[given:]
    (g0, u0, d0, g1, u1, d1), refs = refs[:6], refs[6:]
    o_hbm, refs = refs[:parts], refs[parts:]
    x_ref, bg0, bu0, bd0, bg1, bu1, bd1, gate_ref, hid, o_ref, sems, out_sems = refs
    total, width = o_ref.shape
    ff = g0.shape[1]
    spans = width // span
    each = total // parts
    held = [pl.ds(pl.multiple_of((info[3] ^ p) * each, each), each) if parts > 1 else pl.ds(0, total) for p in range(parts)]
    if given == 1:
        x_copies = [pltpu.make_async_copy(x_hbm[0], x_ref, sems.at[4 + 2 * spans])]
    else:
        x_copies = [pltpu.make_async_copy(x_hbm[p], x_ref.at[held[p]], sems.at[4 + 2 * spans + p]) for p in range(parts)]
    for c in x_copies:
        c.start()
    ins = [pltpu.make_async_copy(src, dst, sems.at[n]) for n, (src, dst) in enumerate(((g0, bg0), (u0, bu0), (g1, bg1), (u1, bu1)))]
    for c in ins:
        c.start()
    downs = []
    for n in range(spans):
        s = pl.ds(n * span, span)
        for m, (src, dst) in enumerate(((d0, bd0), (d1, bd1))):
            downs.append(pltpu.make_async_copy(src.at[:, s], dst.at[:, s], sems.at[4 + 2 * n + m]))
            downs[-1].start()
    for c in x_copies:
        c.wait()

    ids = x_ref[:, width:].astype(F32)
    is_id = lax.broadcasted_iota(jnp.int32, ids.shape, 1) < top
    low, high, flip = info[0].astype(F32), info[1].astype(F32), info[2].astype(F32)
    has_low = jnp.max(jnp.where(is_id & (ids == low), 1.0, 0.0), axis=1, keepdims=True)
    has_high = jnp.max(jnp.where(is_id & (ids == high), 1.0, 0.0), axis=1, keepdims=True)
    share = jnp.broadcast_to(has_low * (1.0 - 0.5 * has_high), (total, 128)).astype(BF16)
    r = lax.broadcasted_iota(jnp.int32, (total, total), 0)
    c = lax.broadcasted_iota(jnp.int32, (total, total), 1)
    same = jnp.where(r // rows == c // rows, 1.0, 0.0).astype(BF16)
    low_rows = jnp.dot(same, share, preferred_element_type=F32)
    at = (lax.broadcasted_iota(jnp.int32, (total, 128), 0) % rows).astype(F32)
    is_low = jnp.where(at < low_rows, 1.0, 0.0)
    first = (is_low * (1.0 - flip) + (1.0 - is_low) * flip)[:, :1]

    for which, (bg, bu) in enumerate(((bg0, bu0), (bg1, bu1))):
        keep = first if which == 0 else 1.0 - first
        ins[2 * which].wait()

        @pl.loop(0, ff // tile)
        def _(t):
            s = pl.ds(pl.multiple_of(t * tile, tile), tile)
            gate_ref[:, s] = jnp.dot(x_ref[:, :width], bg[:, s], preferred_element_type=F32)

        ins[2 * which + 1].wait()

        @pl.loop(0, ff // tile)
        def _(t):
            s = pl.ds(pl.multiple_of(t * tile, tile), tile)
            up = jnp.dot(x_ref[:, :width], bu[:, s], preferred_element_type=F32)
            gate = gate_ref[:, s]
            h = jnp.where(keep > 0.5, gate / (1.0 + jnp.exp(-gate)) * up, 0.0)
            hid[:, pl.ds(pl.multiple_of(which * ff + t * tile, tile), tile)] = h.astype(BF16)

    outs = []
    for n in range(spans):
        downs[2 * n].wait()
        downs[2 * n + 1].wait()
        s = pl.ds(n * span, span)
        o_ref[:, s] = (
            jnp.dot(hid[:, :ff], bd0[:, s], preferred_element_type=F32)
            + jnp.dot(hid[:, ff:], bd1[:, s], preferred_element_type=F32)
        ).astype(BF16)
        for p in range(parts):
            outs.append(pltpu.make_async_copy(o_ref.at[held[p], s], o_hbm[p].at[:, s], out_sems.at[n, p]))
            outs[-1].start()
    for c in outs:
        c.wait()


def experts_apply(info, xs, first, second, parts, rows, top):
    width, ff = first[0].shape
    given = len(xs)
    total = given * xs[0].shape[0]
    each = total // parts
    span = divisor(width // 128, 8) * 128
    spans = width // span
    anywhere = pl.BlockSpec(memory_space=pl.ANY)
    return pl.pallas_call(
        partial(experts_kernel, given=given, parts=parts, rows=rows, top=top, tile=divisor(ff // 128, 2) * 128, span=span),
        out_shape=[jax.ShapeDtypeStruct((each, width), BF16)] * parts,
        grid_spec=pltpu.PrefetchScalarGridSpec(
            num_scalar_prefetch=1,
            grid=(1,),
            in_specs=[anywhere] * (given + 6),
            out_specs=[anywhere] * parts,
            scratch_shapes=[pltpu.VMEM((total, xs[0].shape[1]), BF16)]
            + [pltpu.VMEM(w.shape, BF16) for w in first + second]
            + [pltpu.VMEM((total, ff), F32), pltpu.VMEM((total, 2 * ff), BF16), pltpu.VMEM((total, width), BF16)]
            + [pltpu.SemaphoreType.DMA((4 + 2 * spans + given,)), pltpu.SemaphoreType.DMA((spans, parts))],
        ),
        compiler_params=pltpu.CompilerParams(vmem_limit_bytes=54 * MIB),
        cost_estimate=pl.CostEstimate(
            flops=12 * total * width * ff, bytes_accessed=12 * width * ff + 4 * total * width, transcendentals=2 * total * ff
        ),
    )(info, *xs, *first, *second)


def pack_kernel(tokens, ids, weights, out):
    count, width = tokens.shape
    top = ids.shape[1]
    out[:, :width] = tokens[...]
    hi = weights[...].astype(BF16)
    mid = (weights[...] - hi.astype(F32)).astype(BF16)
    rest = jnp.zeros((count, EXTRA - 3 * top), F32)
    extra = [ids[...].astype(F32), hi.astype(F32), mid.astype(F32), rest]
    out[:, width:] = jnp.concatenate(extra, axis=1).astype(BF16)


def pack(tokens, ids, weights):
    count, width = tokens.shape
    return pl.pallas_call(
        pack_kernel,
        out_shape=jax.ShapeDtypeStruct((count, width + EXTRA), BF16),
        compiler_params=pltpu.CompilerParams(vmem_limit_bytes=16 * MIB),
    )(tokens, ids, weights)


def route_kernel(flag, plane, *refs, choices, sends, relative, rows, top, width):
    blocks, outs, (mix_hi, mix_mid) = refs[:choices], refs[choices : choices + sends], refs[choices + sends :]

    def block(s):
        value = blocks[0][:, s]
        return value if choices == 1 else jnp.where(flag[0] != 0, value, blocks[1][:, s])

    extra = block(slice(width, width + EXTRA)).astype(F32)
    count = extra.shape[0]
    lanes = mix_hi.shape[1]
    ids = plane[:1, :]
    chosen = jnp.zeros((count, 128), F32)
    w_hi, w_mid = chosen, chosen
    for k in range(top):
        same = extra[:, k : k + 1] == ids
        chosen = jnp.where(same, 1.0, chosen)
        w_hi = jnp.where(same, extra[:, top + k : top + k + 1], w_hi)
        w_mid = jnp.where(same, extra[:, 2 * top + k : 2 * top + k + 1], w_mid)

    def table(shape, test):
        r = lax.broadcasted_iota(jnp.int32, shape, 0)
        c = lax.broadcasted_iota(jnp.int32, shape, 1)
        return jnp.where(test(r, c), 1.0, 0.0).astype(BF16)

    def dot(a, b):
        return jnp.dot(a.astype(BF16), b.astype(BF16), preferred_element_type=F32)

    before = table((count, count), lambda r, c: c < r)
    to_high = table((128, 128), lambda r, c: (c == r + 1) & (r % 2 == 0))
    rank = dot(before, chosen) + dot(jnp.ones((count, count), F32), dot(chosen, to_high))
    rank = jnp.where(chosen > 0.0, rank, -1.0)
    at = (lax.broadcasted_iota(jnp.int32, (count, lanes), 1) % rows).astype(F32)
    taken = jnp.zeros((count, lanes), F32)
    sum_hi, sum_mid, taken_back = taken, taken, taken
    for side in range(2):
        spread = table((128, lanes), lambda r, c: r == 2 * (c // rows) + side)
        hit = dot(rank, spread) == at
        taken = jnp.where(hit, 1.0, taken)
        if relative:
            spread = table((128, lanes), lambda r, c: r == 2 * ((c // rows) ^ flag[1]) + side)
            hit = dot(rank, spread) == at
            if sends > 1:
                taken_back = jnp.where(hit, 1.0, taken_back)
        sum_hi = jnp.where(hit, dot(w_hi, spread), sum_hi)
        sum_mid = jnp.where(hit, dot(w_mid, spread), sum_mid)
    mix_hi[...] = sum_hi.astype(BF16)
    mix_mid[...] = sum_mid.astype(BF16)
    taken = (taken_back if sends > 1 else taken).astype(BF16)
    each = lanes // sends
    step = divisor((width + EXTRA) // 128, 11) * 128
    for n in range((width + EXTRA) // step):
        s = slice(n * step, (n + 1) * step)
        got = lax.dot_general(taken, block(s), (((0,), (0,)), ((), ())), preferred_element_type=F32).astype(BF16)
        for p in range(sends):
            outs[p][:, s] = got[p * each : (p + 1) * each]


def route(flag, plane, blocks, sends, relative, rows, top):
    count, wide = blocks[0].shape
    chips = plane.shape[0]
    lanes = chips * rows
    ids = jnp.full((8, 128), -1.0, F32).at[:, : 2 * chips].set(plane.reshape(1, -1))
    whole = pl.BlockSpec(memory_space=pltpu.VMEM)
    out = pl.pallas_call(
        partial(route_kernel, choices=len(blocks), sends=sends, relative=relative, rows=rows, top=top, width=wide - EXTRA),
        in_specs=[pl.BlockSpec(memory_space=pltpu.SMEM), whole] + [whole] * len(blocks),
        out_specs=[whole] * (sends + 2),
        out_shape=[jax.ShapeDtypeStruct((lanes // sends, wide), BF16)] * sends
        + [jax.ShapeDtypeStruct((count, lanes), BF16)] * 2,
        compiler_params=pltpu.CompilerParams(vmem_limit_bytes=24 * MIB),
        cost_estimate=pl.CostEstimate(flops=ROUTE_COST * count * lanes * wide, bytes_accessed=2 * (count + lanes) * wide, transcendentals=0),
    )(flag, ids, *blocks)
    return out[:sends], out[sends:]


def mix_kernel(hi, mid, *refs, parts, terms):
    backs, refs = refs[:parts], refs[parts:]
    adds, outs = refs[: len(refs) - len(terms)], refs[len(refs) - len(terms) :]
    rows = jnp.concatenate([b[...] for b in backs], axis=0)
    total = jnp.dot(hi[...], rows, preferred_element_type=F32) + jnp.dot(mid[...], rows, preferred_element_type=F32)
    for (with_total, used), out in zip(terms, outs):
        value = total if with_total else None
        for n in used:
            add = adds[n][...].astype(F32)
            value = add if value is None else value + add
        out[...] = value.astype(out.dtype)


def mix_rows(mix, backs, adds, terms, dtypes):
    count, lanes = mix[0].shape
    width = backs[0].shape[1]
    step = divisor(width // 128, 8) * 128
    full = pl.BlockSpec((count, lanes), lambda n: (0, 0))
    tall = pl.BlockSpec((count, step), lambda n: (0, n))
    return pl.pallas_call(
        partial(mix_kernel, parts=len(backs), terms=tuple(terms)),
        grid=(width // step,),
        in_specs=[full, full] + [pl.BlockSpec((b.shape[0], step), lambda n: (0, n)) for b in backs] + [tall] * len(adds),
        out_specs=[tall] * len(terms),
        out_shape=[jax.ShapeDtypeStruct((count, width), d) for d in dtypes],
        compiler_params=pltpu.CompilerParams(vmem_limit_bytes=24 * MIB),
        cost_estimate=pl.CostEstimate(flops=MIX_COST * count * lanes * width, bytes_accessed=6 * count * width, transcendentals=0),
    )(*mix, *backs, *adds)


def after(value, *others):
    return lax.optimization_barrier((value,) + others)[0]


def local(tokens, router_weights, expert_ids, gate_weight, up_weight, down_weight):
    z_size = lax.axis_size("z")
    x_size = lax.axis_size("x")
    y_size = lax.axis_size("y")
    lane_count = z_size * x_size
    chips = y_size * x_size
    count, width = tokens.shape
    top = expert_ids.shape[1]
    rows = count * top // (y_size * lane_count)
    z_at = lax.axis_index("z")

    parts = chips if chips in (2, 4) else 1
    here = lax.axis_index("y") * x_size + lax.axis_index("x")
    chip = jnp.arange(chips, dtype=jnp.int32)
    low = 2 * (chip // x_size) * lane_count + z_at * x_size + chip % x_size
    plane = jnp.stack([low, low + lane_count], axis=-1).astype(F32)
    low_here = 2 * lax.axis_index("y") * lane_count + z_at * x_size + lax.axis_index("x")
    info = jnp.stack([low_here, low_here + lane_count, lax.axis_index("core"), here]).astype(jnp.int32)

    def flip(value, mask):
        return lax.ppermute(value, "z", [(i, i ^ mask) for i in range(z_size)])

    def inner(value):
        return lax.ppermute(value, "z", [(1, 2), (2, 1)])

    def outward(value):
        return lax.ppermute(value, "z", [(1, 0), (2, 3)])

    def inward(value):
        return lax.ppermute(value, "z", [(0, 1), (3, 2)])

    is_end = (z_at == 0) | (z_at == z_size - 1)

    block = pack(tokens, expert_ids, router_weights)
    flag = jnp.stack([is_end.astype(jnp.int32), here])
    swap = [(0, 1), (1, 0)]
    own = [gate_weight[0], up_weight[0], down_weight[0]]
    other = [lax.ppermute(w, "core", swap) for w in own]

    def exchange(values):
        if len(values) == 1:
            value = values[0].reshape(chips, rows, values[0].shape[1])
            return [lax.all_to_all(value, ("y", "x"), 0, 0, tiled=True).reshape(values[0].shape)]
        pairs = [[(i, i ^ m) for i in range(chips)] for m in range(chips)]
        return [values[0]] + [lax.ppermute(values[m], ("y", "x"), pairs[m]) for m in range(1, chips)]

    def run(k, *others):
        outs[k] = experts_apply(info, after(arrived[k], *others), own, other, parts, rows, top)

    line = z_size == 4
    moving = {k: flip(block, k) for k in ((1,) if line else range(1, z_size)) if k & (k - 1) == 0}
    if line:
        middle = inner(block)
    held, mixes, sent, arrived, outs = {0: [block]}, {}, {}, {}, {}
    for k in range(z_size):
        if k and line:
            if k == 1:
                held[1] = [after(moving[1], sent[0])]
                next_inner, next_outer = inner(held[1][0]), outward(after(middle, sent[0]))
            elif k == 2:
                passed = after(next_inner, sent[1])
                last_outer = outward(passed)
                held[2] = [next_outer, passed]
            else:
                held[3] = [after(last_outer, outs[0]), middle]
        elif k:
            bit = k & -k
            held[k] = [after(moving[k] if k == bit else flip(held[k ^ bit][0], bit), sent[k - 1])]
        sends = parts if k in PERMUTED else 1
        sent[k], mixes[k] = route(flag, plane, held[k], sends, parts > 1, rows, top)
        if k:
            sent[k] = after(sent[k], arrived[k - 1])
        if k > 1:
            run(k - 2, sent[k])
        arrived[k] = exchange(sent[k])
    last = z_size - 1
    run(last, *[outs[o] for o in outs])

    back, hold, extra = None, [], []
    for k in range(last, -1, -1):
        source = outs[k] if k == last else after(outs[k], *hold, *(back if parts == 1 else []))
        if k < last:
            done = k + 1
            got = after(back, source)
            if not line:
                bit = done & -done
                adds = [r for o, r in extra if o == done]
                hold = mix_rows(mixes[done], got, adds, [(True, range(len(adds)))], [BF16])
                extra.append((done ^ bit, flip(hold[0], bit)))
            elif done == 3:
                third, total = mix_rows(mixes[3], got, [], [(True, ()), (True, ())], [F32, BF16])
                hold = [total]
                from_end = inward(total)
            elif done == 2:
                hold = mix_rows(mixes[2], got, [from_end], [(True, ()), (True, (0,))], [BF16] * 2)
                near, far = inward(hold[0]), inner(hold[1])
            else:
                hold = mix_rows(mixes[1], got, [far, third, near], [(True, (0,)), (False, (1, 2))], [BF16] * 2)
                extra += [(0, flip(hold[0], 1)), (0, inner(hold[1]))]
        if k and k - 1 not in outs:
            run(k - 1, source, *hold)
        back = exchange(source)
    adds = [r for o, r in extra if o == 0]
    return mix_rows(mixes[0], back, adds, [(True, range(len(adds)))], [BF16])[0]


def solution(mesh):
    groups, lanes = mesh.shape["dp"], mesh.shape["expert"]
    y_size = groups // 2
    x_size = y_size if lanes % y_size == 0 else 1
    fine = Mesh(mesh.devices.reshape(y_size, 2, lanes // x_size, x_size), ("y", "core", "z", "x"))
    split = ("y", "core", "z", "x")
    flat, deep = P(split, None), P(split, None, None)
    return jax.shard_map(
        local, mesh=fine, in_specs=(flat, flat, flat, deep, deep, deep), out_specs=flat, check_vma=False
    )
```

```python
from functools import partial

import jax
import jax.numpy as jnp
from jax import lax
from jax.experimental import pallas as pl
from jax.experimental.pallas import tpu as pltpu
from jax.sharding import Mesh, PartitionSpec as P

F32 = jnp.float32
BF16 = jnp.bfloat16
EXTRA = 128
MIB = 2**20
PERMUTED = (2, 3)
ROUTE_COST = 400
MIX_COST = 4


def divisor(size, most):
    return next(d for d in range(min(size, most), 0, -1) if size % d == 0)


def experts_kernel(info, *refs, given, parts, rows, top, tile, span):
    x_hbm, refs = refs[:given], refs[given:]
    (g0, u0, d0, g1, u1, d1), refs = refs[:6], refs[6:]
    o_hbm, refs = refs[:parts], refs[parts:]
    x_ref, bg0, bu0, bd0, bg1, bu1, bd1, gate_ref, hid, o_ref, sems, out_sems = refs
    total, width = o_ref.shape
    ff = g0.shape[1]
    spans = width // span
    each = total // parts
    held = [pl.ds(pl.multiple_of((info[3] ^ p) * each, each), each) if parts > 1 else pl.ds(0, total) for p in range(parts)]
    if given == 1:
        x_copies = [pltpu.make_async_copy(x_hbm[0], x_ref, sems.at[4 + 2 * spans])]
    else:
        x_copies = [pltpu.make_async_copy(x_hbm[p], x_ref.at[held[p]], sems.at[4 + 2 * spans + p]) for p in range(parts)]
    for c in x_copies:
        c.start()
    ins = [pltpu.make_async_copy(src, dst, sems.at[n]) for n, (src, dst) in enumerate(((g0, bg0), (u0, bu0), (g1, bg1), (u1, bu1)))]
    for c in ins:
        c.start()
    downs = []
    for n in range(spans):
        s = pl.ds(n * span, span)
        for m, (src, dst) in enumerate(((d0, bd0), (d1, bd1))):
            downs.append(pltpu.make_async_copy(src.at[:, s], dst.at[:, s], sems.at[4 + 2 * n + m]))
            downs[-1].start()
    for c in x_copies:
        c.wait()

    ids = x_ref[:, width:].astype(F32)
    is_id = lax.broadcasted_iota(jnp.int32, ids.shape, 1) < top
    low, high, flip = info[0].astype(F32), info[1].astype(F32), info[2].astype(F32)
    has_low = jnp.max(jnp.where(is_id & (ids == low), 1.0, 0.0), axis=1, keepdims=True)
    has_high = jnp.max(jnp.where(is_id & (ids == high), 1.0, 0.0), axis=1, keepdims=True)
    share = jnp.broadcast_to(has_low * (1.0 - 0.5 * has_high), (total, 128)).astype(BF16)
    r = lax.broadcasted_iota(jnp.int32, (total, total), 0)
    c = lax.broadcasted_iota(jnp.int32, (total, total), 1)
    same = jnp.where(r // rows == c // rows, 1.0, 0.0).astype(BF16)
    low_rows = jnp.dot(same, share, preferred_element_type=F32)
    at = (lax.broadcasted_iota(jnp.int32, (total, 128), 0) % rows).astype(F32)
    is_low = jnp.where(at < low_rows, 1.0, 0.0)
    first = (is_low * (1.0 - flip) + (1.0 - is_low) * flip)[:, :1]

    for which, (bg, bu) in enumerate(((bg0, bu0), (bg1, bu1))):
        keep = first if which == 0 else 1.0 - first
        ins[2 * which].wait()

        @pl.loop(0, ff // tile)
        def _(t):
            s = pl.ds(pl.multiple_of(t * tile, tile), tile)
            gate_ref[:, s] = jnp.dot(x_ref[:, :width], bg[:, s], preferred_element_type=F32)

        ins[2 * which + 1].wait()

        @pl.loop(0, ff // tile)
        def _(t):
            s = pl.ds(pl.multiple_of(t * tile, tile), tile)
            up = jnp.dot(x_ref[:, :width], bu[:, s], preferred_element_type=F32)
            gate = gate_ref[:, s]
            h = jnp.where(keep > 0.5, gate / (1.0 + jnp.exp(-gate)) * up, 0.0)
            hid[:, pl.ds(pl.multiple_of(which * ff + t * tile, tile), tile)] = h.astype(BF16)

    outs = []
    for n in range(spans):
        downs[2 * n].wait()
        downs[2 * n + 1].wait()
        s = pl.ds(n * span, span)
        o_ref[:, s] = (
            jnp.dot(hid[:, :ff], bd0[:, s], preferred_element_type=F32)
            + jnp.dot(hid[:, ff:], bd1[:, s], preferred_element_type=F32)
        ).astype(BF16)
        for p in range(parts):
            outs.append(pltpu.make_async_copy(o_ref.at[held[p], s], o_hbm[p].at[:, s], out_sems.at[n, p]))
            outs[-1].start()
    for c in outs:
        c.wait()


def experts_apply(info, xs, first, second, parts, rows, top):
    width, ff = first[0].shape
    given = len(xs)
    total = given * xs[0].shape[0]
    each = total // parts
    span = divisor(width // 128, 8) * 128
    spans = width // span
    anywhere = pl.BlockSpec(memory_space=pl.ANY)
    return pl.pallas_call(
        partial(experts_kernel, given=given, parts=parts, rows=rows, top=top, tile=divisor(ff // 128, 2) * 128, span=span),
        out_shape=[jax.ShapeDtypeStruct((each, width), BF16)] * parts,
        grid_spec=pltpu.PrefetchScalarGridSpec(
            num_scalar_prefetch=1,
            grid=(1,),
            in_specs=[anywhere] * (given + 6),
            out_specs=[anywhere] * parts,
            scratch_shapes=[pltpu.VMEM((total, xs[0].shape[1]), BF16)]
            + [pltpu.VMEM(w.shape, BF16) for w in first + second]
            + [pltpu.VMEM((total, ff), F32), pltpu.VMEM((total, 2 * ff), BF16), pltpu.VMEM((total, width), BF16)]
            + [pltpu.SemaphoreType.DMA((4 + 2 * spans + given,)), pltpu.SemaphoreType.DMA((spans, parts))],
        ),
        compiler_params=pltpu.CompilerParams(vmem_limit_bytes=54 * MIB),
        cost_estimate=pl.CostEstimate(
            flops=12 * total * width * ff, bytes_accessed=12 * width * ff + 4 * total * width, transcendentals=2 * total * ff
        ),
    )(info, *xs, *first, *second)


def pack_kernel(tokens, ids, weights, out):
    count, width = tokens.shape
    top = ids.shape[1]
    out[:, :width] = tokens[...]
    hi = weights[...].astype(BF16)
    mid = (weights[...] - hi.astype(F32)).astype(BF16)
    rest = jnp.zeros((count, EXTRA - 3 * top), F32)
    extra = [ids[...].astype(F32), hi.astype(F32), mid.astype(F32), rest]
    out[:, width:] = jnp.concatenate(extra, axis=1).astype(BF16)


def pack(tokens, ids, weights):
    count, width = tokens.shape
    return pl.pallas_call(
        pack_kernel,
        out_shape=jax.ShapeDtypeStruct((count, width + EXTRA), BF16),
        compiler_params=pltpu.CompilerParams(vmem_limit_bytes=16 * MIB),
    )(tokens, ids, weights)


def route_kernel(flag, *refs, choices, sends, relative, rows, top, width, sizes):
    blocks, outs, (mix_hi, mix_mid) = refs[:choices], refs[choices : choices + sends], refs[choices + sends :]

    def block(s):
        value = blocks[0][:, s]
        return value if choices == 1 else jnp.where(flag[0] != 0, value, blocks[1][:, s])

    extra = block(slice(width, width + EXTRA)).astype(F32)
    count = extra.shape[0]
    lanes = mix_hi.shape[1]
    chips, x_size, lane_count = sizes
    lane = lax.broadcasted_iota(jnp.int32, (1, 128), 1)
    chip = lane // 2
    ids = 2 * (chip // x_size) * lane_count + flag[2] * x_size + chip % x_size + lane % 2 * lane_count
    ids = jnp.where(lane < 2 * chips, ids, -1).astype(F32)
    chosen = jnp.zeros((count, 128), F32)
    w_hi, w_mid = chosen, chosen
    for k in range(top):
        same = extra[:, k : k + 1] == ids
        chosen = jnp.where(same, 1.0, chosen)
        w_hi = jnp.where(same, extra[:, top + k : top + k + 1], w_hi)
        w_mid = jnp.where(same, extra[:, 2 * top + k : 2 * top + k + 1], w_mid)

    def table(shape, test):
        r = lax.broadcasted_iota(jnp.int32, shape, 0)
        c = lax.broadcasted_iota(jnp.int32, shape, 1)
        return jnp.where(test(r, c), 1.0, 0.0).astype(BF16)

    def dot(a, b):
        return jnp.dot(a.astype(BF16), b.astype(BF16), preferred_element_type=F32)

    before = table((count, count), lambda r, c: c < r)
    to_high = table((128, 128), lambda r, c: (c == r + 1) & (r % 2 == 0))
    rank = dot(before, chosen) + dot(jnp.ones((count, count), F32), dot(chosen, to_high))
    rank = jnp.where(chosen > 0.0, rank, -1.0)
    at = (lax.broadcasted_iota(jnp.int32, (count, lanes), 1) % rows).astype(F32)
    taken = jnp.zeros((count, lanes), F32)
    sum_hi, sum_mid, taken_back = taken, taken, taken
    for side in range(2):
        spread = table((128, lanes), lambda r, c: r == 2 * (c // rows) + side)
        hit = dot(rank, spread) == at
        taken = jnp.where(hit, 1.0, taken)
        if relative:
            spread = table((128, lanes), lambda r, c: r == 2 * ((c // rows) ^ flag[1]) + side)
            hit = dot(rank, spread) == at
            if sends > 1:
                taken_back = jnp.where(hit, 1.0, taken_back)
        sum_hi = jnp.where(hit, dot(w_hi, spread), sum_hi)
        sum_mid = jnp.where(hit, dot(w_mid, spread), sum_mid)
    mix_hi[...] = sum_hi.astype(BF16)
    mix_mid[...] = sum_mid.astype(BF16)
    taken = (taken_back if sends > 1 else taken).astype(BF16)
    each = lanes // sends
    step = divisor((width + EXTRA) // 128, 11) * 128
    for n in range((width + EXTRA) // step):
        s = slice(n * step, (n + 1) * step)
        got = lax.dot_general(taken, block(s), (((0,), (0,)), ((), ())), preferred_element_type=F32).astype(BF16)
        for p in range(sends):
            outs[p][:, s] = got[p * each : (p + 1) * each]


def route(flag, sizes, blocks, sends, relative, rows, top):
    count, wide = blocks[0].shape
    lanes = sizes[0] * rows
    whole = pl.BlockSpec(memory_space=pltpu.VMEM)
    out = pl.pallas_call(
        partial(route_kernel, choices=len(blocks), sends=sends, relative=relative, rows=rows, top=top, width=wide - EXTRA, sizes=sizes),
        in_specs=[pl.BlockSpec(memory_space=pltpu.SMEM)] + [whole] * len(blocks),
        out_specs=[whole] * (sends + 2),
        out_shape=[jax.ShapeDtypeStruct((lanes // sends, wide), BF16)] * sends
        + [jax.ShapeDtypeStruct((count, lanes), BF16)] * 2,
        compiler_params=pltpu.CompilerParams(vmem_limit_bytes=24 * MIB),
        cost_estimate=pl.CostEstimate(flops=ROUTE_COST * count * lanes * wide, bytes_accessed=2 * (count + lanes) * wide, transcendentals=0),
    )(flag, *blocks)
    return out[:sends], out[sends:]


def mix_kernel(hi, mid, *refs, parts, terms):
    backs, refs = refs[:parts], refs[parts:]
    adds, outs = refs[: len(refs) - len(terms)], refs[len(refs) - len(terms) :]
    rows = jnp.concatenate([b[...] for b in backs], axis=0)
    total = jnp.dot(hi[...], rows, preferred_element_type=F32) + jnp.dot(mid[...], rows, preferred_element_type=F32)
    for (with_total, used), out in zip(terms, outs):
        value = total if with_total else None
        for n in used:
            add = adds[n][...].astype(F32)
            value = add if value is None else value + add
        out[...] = value.astype(out.dtype)


def mix_rows(mix, backs, adds, terms, dtypes):
    count, lanes = mix[0].shape
    width = backs[0].shape[1]
    step = divisor(width // 128, 8) * 128
    full = pl.BlockSpec((count, lanes), lambda n: (0, 0))
    tall = pl.BlockSpec((count, step), lambda n: (0, n))
    return pl.pallas_call(
        partial(mix_kernel, parts=len(backs), terms=tuple(terms)),
        grid=(width // step,),
        in_specs=[full, full] + [pl.BlockSpec((b.shape[0], step), lambda n: (0, n)) for b in backs] + [tall] * len(adds),
        out_specs=[tall] * len(terms),
        out_shape=[jax.ShapeDtypeStruct((count, width), d) for d in dtypes],
        compiler_params=pltpu.CompilerParams(vmem_limit_bytes=24 * MIB),
        cost_estimate=pl.CostEstimate(flops=MIX_COST * count * lanes * width, bytes_accessed=6 * count * width, transcendentals=0),
    )(*mix, *backs, *adds)


def after(value, *others):
    return lax.optimization_barrier((value,) + others)[0]


def local(tokens, router_weights, expert_ids, gate_weight, up_weight, down_weight):
    z_size = lax.axis_size("z")
    x_size = lax.axis_size("x")
    y_size = lax.axis_size("y")
    lane_count = z_size * x_size
    chips = y_size * x_size
    count, width = tokens.shape
    top = expert_ids.shape[1]
    rows = count * top // (y_size * lane_count)
    z_at = lax.axis_index("z")

    parts = chips if chips in (2, 4) else 1
    here = lax.axis_index("y") * x_size + lax.axis_index("x")
    low_here = 2 * lax.axis_index("y") * lane_count + z_at * x_size + lax.axis_index("x")
    info = jnp.stack([low_here, low_here + lane_count, lax.axis_index("core"), here]).astype(jnp.int32)

    def flip(value, mask):
        return lax.ppermute(value, "z", [(i, i ^ mask) for i in range(z_size)])

    def inner(value):
        return lax.ppermute(value, "z", [(1, 2), (2, 1)])

    def outward(value):
        return lax.ppermute(value, "z", [(1, 0), (2, 3)])

    def inward(value):
        return lax.ppermute(value, "z", [(0, 1), (3, 2)])

    is_end = (z_at == 0) | (z_at == z_size - 1)

    block = pack(tokens, expert_ids, router_weights)
    flag = jnp.stack([is_end.astype(jnp.int32), here, z_at])
    swap = [(0, 1), (1, 0)]
    own = [gate_weight[0], up_weight[0], down_weight[0]]
    other = [lax.ppermute(w, "core", swap) for w in own]

    def exchange(values):
        if len(values) == 1:
            value = values[0].reshape(chips, rows, values[0].shape[1])
            return [lax.all_to_all(value, ("y", "x"), 0, 0, tiled=True).reshape(values[0].shape)]
        pairs = [[(i, i ^ m) for i in range(chips)] for m in range(chips)]
        return [values[0]] + [lax.ppermute(values[m], ("y", "x"), pairs[m]) for m in range(1, chips)]

    def run(k, *others):
        outs[k] = experts_apply(info, after(arrived[k], *others), own, other, parts, rows, top)

    line = z_size == 4
    moving = {k: flip(block, k) for k in ((1,) if line else range(1, z_size)) if k & (k - 1) == 0}
    if line:
        middle = inner(block)
    held, mixes, sent, arrived, outs = {0: [block]}, {}, {}, {}, {}
    for k in range(z_size):
        if k and line:
            if k == 1:
                held[1] = [after(moving[1], sent[0])]
                next_inner, next_outer = inner(held[1][0]), outward(after(middle, sent[0]))
            elif k == 2:
                passed = after(next_inner, sent[1])
                last_outer = outward(passed)
                held[2] = [next_outer, passed]
            else:
                held[3] = [after(last_outer, outs[0]), middle]
        elif k:
            bit = k & -k
            held[k] = [after(moving[k] if k == bit else flip(held[k ^ bit][0], bit), sent[k - 1])]
        sends = parts if k in PERMUTED else 1
        sent[k], mixes[k] = route(flag, (chips, x_size, lane_count), held[k], sends, parts > 1, rows, top)
        if k:
            sent[k] = after(sent[k], arrived[k - 1])
        if k > 1:
            run(k - 2, sent[k])
        arrived[k] = exchange(sent[k])
    last = z_size - 1
    run(last, *[outs[o] for o in outs])

    back, hold, extra = None, [], []
    for k in range(last, -1, -1):
        source = outs[k] if k == last else after(outs[k], *hold, *(back if parts == 1 else []))
        if k < last:
            done = k + 1
            got = after(back, source)
            if not line:
                bit = done & -done
                adds = [r for o, r in extra if o == done]
                hold = mix_rows(mixes[done], got, adds, [(True, range(len(adds)))], [BF16])
                extra.append((done ^ bit, flip(hold[0], bit)))
            elif done == 3:
                third, total = mix_rows(mixes[3], got, [], [(True, ()), (True, ())], [F32, BF16])
                hold = [total]
                from_end = inward(total)
            elif done == 2:
                hold = mix_rows(mixes[2], got, [from_end], [(True, ()), (True, (0,))], [BF16] * 2)
                near, far = inward(hold[0]), inner(hold[1])
            else:
                hold = mix_rows(mixes[1], got, [far, third, near], [(True, (0,)), (False, (1, 2))], [BF16] * 2)
                extra += [(0, flip(hold[0], 1)), (0, inner(hold[1]))]
        if k and k - 1 not in outs:
            run(k - 1, source, *hold)
        back = exchange(source)
    adds = [r for o, r in extra if o == 0]
    return mix_rows(mixes[0], back, adds, [(True, range(len(adds)))], [BF16])[0]


def solution(mesh):
    groups, lanes = mesh.shape["dp"], mesh.shape["expert"]
    y_size = groups // 2
    x_size = y_size if lanes % y_size == 0 else 1
    fine = Mesh(mesh.devices.reshape(y_size, 2, lanes // x_size, x_size), ("y", "core", "z", "x"))
    split = ("y", "core", "z", "x")
    flat, deep = P(split, None), P(split, None, None)
    return jax.shard_map(
        local, mesh=fine, in_specs=(flat, flat, flat, deep, deep, deep), out_specs=flat, check_vma=False
    )
```
